512 devices in a mesh: slab: 128 (over z, y, core), coil: 4 (over x).
Axes of the slice: x: 4, y: 8, z: 8, core: 2. Of those that a mesh axis runs over, the one named last changes fastest.
Arguments:
- iterate: float32 [2, 4, 4, 384, 384], P(None, 'coil', None, 'slab'), may hold values from -6 to 6
- residual: float32 [2, 4, 4, 384, 384], P(None, 'coil', None, 'slab'), may hold values from -50 to 50
- direction: float32 [2, 4, 4, 384, 384], P(None, 'coil', None, 'slab'), may hold values from -50 to 50
- sensitivity: bfloat16 [2, 32, 4, 384, 384], P(None, 'coil', None, 'slab'), may hold values from -0.75 to 0.75
- sampling: int32 [4, 384, 384], replicated, may hold values from 0 to 1
- edge_weight: int32 [4, 4, 384, 384], P('coil', None, 'slab'), may hold values from 1 to 4
Outputs:
- new_iterate: float32 [2, 4, 4, 384, 384], P(None, 'coil', None, 'slab')
- new_residual: float32 [2, 4, 4, 384, 384], P(None, 'coil', None, 'slab')
- new_direction: float32 [2, 4, 4, 384, 384], P(None, 'coil', None, 'slab')
- new_norm: float32 [], replicated
The draws below stay inside these ranges and needn't reach their ends.
All inputs are finite; a program needn't handle non-finite values.
Results may differ from the reference program's by a relative error of at most 0.0013.
Values sent between devices are 32-bit elements; how exact they have to be, the bound alone decides.
No kernel may reach another device: no remote copies, remote signals or barrier semaphores. Data moves between devices by JAX's collectives and lax.ppermute only.
A program may use at most 64 MiB of HBM per device.

```python
import math
import jax
import jax.numpy as jnp
from jax import lax

C = 32
X = 384
Y = 384
F = 4
Z = 4


def scaled_field(noise, col_key):
    position = jnp.arange(X, dtype=jnp.float32) / (X - 1)
    col_draw = jax.random.uniform(col_key, (Y,), jnp.float32)
    row_scale = 10.0 ** (position - 0.5)
    col_scale = 10.0 ** (col_draw - 0.5)
    return noise * row_scale[:, None] * col_scale


def draw_direction(key, part):
    key = jax.random.fold_in(key, 11)
    base_key, col_key = jax.random.split(key)
    extents = (2, F, Z, X, Y)
    noise = jnp.clip(jax.random.normal(base_key, extents, jnp.float32), -5.0, 5.0)
    return scaled_field(noise, col_key)


def draw_residual(key, part):
    key = jax.random.fold_in(key, 23)
    base_key, col_key = jax.random.split(key)
    extents = (2, F, Z, X, Y)
    noise = jnp.clip(jax.random.normal(base_key, extents, jnp.float32), -5.0, 5.0)
    return scaled_field(noise, col_key)


def draw_sampling(key, part):
    key = jax.random.fold_in(key, 37)
    row_freq = jnp.arange(X, dtype=jnp.int32)
    col_freq = jnp.arange(Y, dtype=jnp.int32)
    row_dist = jnp.minimum(row_freq, X - row_freq) * 1024 // (X // 2)
    col_dist = jnp.minimum(col_freq, Y - col_freq) * 1024 // (Y // 2)
    radius = jnp.maximum(row_dist[:, None], col_dist[None, :])
    density = jnp.maximum(128, 1024 - radius)
    tickets = jax.random.randint(key, (F, X, Y), 0, 1024, dtype=jnp.int32)
    return (tickets < density[None]).astype(jnp.int32)


def touch_ends(drawn, own_key, least, high):
    shape = drawn.shape
    place = [jax.random.randint(jax.random.fold_in(own_key, axis), (), 0, shape[axis]) for axis in range(len(shape))]
    drawn = drawn.at[tuple(place)].set(least)
    longest = shape.index(max(shape))
    place[longest] = (place[longest] + 1) % shape[longest]
    return drawn.at[tuple(place)].set(high)


def levels(rng, dims, cuts, low, largest):
    def one(dim, parts):
        heights = jax.random.uniform(jax.random.fold_in(jax.random.fold_in(rng, 6), dim), (parts,), jnp.float32, low / len(cuts), largest / len(cuts))
        return jnp.repeat(jnp.exp(heights), dims[dim] // parts).reshape((-1,) + (1,) * (len(dims) - dim - 1))

    loudness = one(*cuts[0])
    for cut in cuts[1:]:
        loudness = loudness * one(*cut)
    return loudness


def normal_values(own_key, dims, scale, most, pieces=(), kind=jnp.bfloat16):
    gain = levels(own_key, dims, pieces, -0.22, 0.18) if pieces else 1.0
    values = jax.random.normal(own_key, dims, jnp.float32) * scale * gain
    return jnp.minimum(jnp.maximum(values, -most), most).astype(kind)


def setup_inputs(seed: int = 0) -> dict:
    key_of = jax.random.split(jax.random.key(seed), 7)
    return {
        "iterate": normal_values(key_of[0], (2, F, Z, X, Y), 1.0, 6.0, ((1, 4), (3, 128)), jnp.float32),
        "residual": draw_residual(jax.random.fold_in(key_of[6], 71), 0),
        "direction": draw_direction(jax.random.fold_in(key_of[6], 71), 0),
        "sensitivity": normal_values(key_of[3], (2, C, Z, X, Y), 0.125, 0.75, ((1, 4), (3, 128))),
        "sampling": draw_sampling(jax.random.fold_in(key_of[6], 71), 0),
        "edge_weight": touch_ends(jax.random.randint(key_of[5], (F, Z, X, Y), 1, 5), jax.random.fold_in(key_of[5], 1), 1, 4).astype(jnp.int32),
    }


smooth_scale = 0.05

def dft_tables(length):
    counter = jnp.arange(length, dtype=jnp.int32)
    phases = counter[:, None] * counter[None, :] % length
    angles = phases.astype(jnp.float32) * (2.0 * math.pi / length)
    unit_norm = 1.0 / math.sqrt(length)
    return ((jnp.cos(angles) * unit_norm).astype(jnp.bfloat16), (jnp.sin(angles) * unit_norm).astype(jnp.bfloat16))

def rejoined(values):
    upper = lax.optimization_barrier(values.astype(jnp.bfloat16))
    lower = (values - upper.astype(jnp.float32)).astype(jnp.bfloat16)
    return upper.astype(jnp.float32) + lower.astype(jnp.float32)

def last_product(values, matrix):
    extents = values.shape
    flat = values.reshape(-1, extents[-1])
    result = jnp.dot(flat, matrix.astype(jnp.float32), precision=lax.Precision.HIGHEST)
    return result.reshape(extents[:-1] + (matrix.shape[1],))

def spin(field, axis, cos_table, sin_table, orient):
    moved = jnp.swapaxes(field, axis, -1)
    real_part = rejoined(moved[0])
    imag_part = rejoined(moved[1])
    real_out = last_product(real_part, cos_table) + orient * last_product(imag_part, sin_table)
    imag_out = last_product(imag_part, cos_table) - orient * last_product(real_part, sin_table)
    return jnp.swapaxes(jnp.stack([real_out, imag_out]), axis, -1)

def edge_term(field, weight, axis):
    extent = field.shape[axis]
    onward = jnp.concatenate([lax.slice_in_dim(field, 1, extent, axis=axis), jnp.zeros_like(lax.slice_in_dim(field, 0, 1, axis=axis))], axis)
    position = lax.broadcasted_iota(jnp.int32, field.shape, axis)
    flux_term = jnp.where(position < extent - 1, onward - field, 0.0) * weight
    earlier = jnp.concatenate([jnp.zeros_like(lax.slice_in_dim(flux_term, 0, 1, axis=axis)), lax.slice_in_dim(flux_term, 0, extent - 1, axis=axis)], axis)
    return earlier - flux_term

def reference(iterate, residual, direction, sensitivity, sampling, edge_weight):
    cos_cols, sin_cols = dft_tables(Y)
    cos_rows, sin_rows = dft_tables(X)
    dir_real = direction[0]
    dir_imag = direction[1]
    frame_mask = sampling.astype(jnp.float32)[None, :, None, :, :]

    def one_coil(summed, coil_sens):
        sens_real = coil_sens[0].astype(jnp.float32)[None]
        sens_imag = coil_sens[1].astype(jnp.float32)[None]
        images = jnp.stack([sens_real * dir_real - sens_imag * dir_imag, sens_real * dir_imag + sens_imag * dir_real])
        spectrum = spin(spin(images, -1, cos_cols, sin_cols, 1.0), -2, cos_rows, sin_rows, 1.0)
        spectrum = spectrum * frame_mask
        back = spin(spin(spectrum, -2, cos_rows, sin_rows, -1.0), -1, cos_cols, sin_cols, -1.0)
        back_real = back[0]
        back_imag = back[1]
        term = jnp.stack([sens_real * back_real + sens_imag * back_imag, sens_real * back_imag - sens_imag * back_real])
        return (summed + term, None)
    data_term, _ = lax.scan(one_coil, jnp.zeros_like(direction), jnp.moveaxis(sensitivity, 1, 0))
    weight = edge_weight.astype(jnp.float32)[None]
    smooth = jnp.zeros_like(direction)
    for axis_index in range(1, 5):
        smooth = smooth + edge_term(direction, weight, axis_index)
    applied = data_term + smooth_scale * smooth
    old_norm = jnp.sum(residual * residual)
    curvature = jnp.sum(direction * applied)
    step_size = old_norm / curvature
    new_iterate = iterate + step_size * direction
    new_residual = residual - step_size * applied
    new_norm = jnp.sum(new_residual * new_residual)
    new_direction = new_residual + new_norm / old_norm * direction
    return (new_iterate, new_residual, new_direction, new_norm)
```

```python
import functools
import math

import jax
import jax.numpy as jnp
import ml_dtypes
import numpy as np
from jax import lax
from jax.experimental import pallas as pl
from jax.experimental.pallas import tpu as pltpu
from jax.sharding import Mesh
from jax.sharding import PartitionSpec as P

smooth_scale = 0.05
slab_axes = ("z", "y", "core")
f32 = jnp.float32
bf16 = jnp.bfloat16

first_rows = 18
second_rows = 20


def dft_tables(length):
    counter = np.arange(length, dtype=np.int64)
    phases = (counter[:, None] * counter[None, :]) % length
    angles = phases.astype(np.float32) * np.float32(2.0 * math.pi / length)
    unit_norm = np.float32(1.0 / math.sqrt(length))
    wide = angles.astype(np.float64)
    cos = np.cos(wide).astype(np.float32) * unit_norm
    sin = np.sin(wide).astype(np.float32) * unit_norm
    return cos.astype(ml_dtypes.bfloat16), sin.astype(ml_dtypes.bfloat16)


def split(values):
    upper = values.astype(bf16)
    return upper, (values - upper.astype(f32)).astype(bf16)


def mm(a, b, contract):
    return lax.dot_general(a, b, (contract, ((), ())), preferred_element_type=f32)


def sens_rows(sens_ref, part, row, coils):
    pieces = [sens_ref[part, c, row].astype(f32) for c in range(coils)]
    return jnp.concatenate(pieces, axis=0)


def images_kernel(sens_ref, field_ref, table_ref, out_ref):
    coils, rows = sens_ref.shape[1], sens_ref.shape[2]
    frames = field_ref.shape[0]
    table = table_ref[...]
    table = jnp.concatenate([table, table], axis=1)
    half = table.shape[0] // 2
    for r in range(rows):
        s_re = sens_rows(sens_ref, 0, r, coils)
        s_im = sens_rows(sens_ref, 1, r, coils)
        real, imag = [], []
        for f in range(frames):
            d_re = jnp.concatenate([field_ref[f, 0, r]] * coils, axis=0)
            d_im = jnp.concatenate([field_ref[f, 1, r]] * coils, axis=0)
            real.append(s_re * d_re - s_im * d_im)
            imag.append(s_re * d_im + s_im * d_re)
        upper, lower = split(jnp.concatenate(real + imag, axis=0))
        got = mm(table, jnp.concatenate([upper, lower], axis=1), ((1,), (1,)))
        re = got[:half, :128] + got[half:, 128:]
        im = got[:half, 128:] - got[half:, :128]
        for j in range(half // 128):
            at = (j * rows + r) * 2
            out_ref[pl.ds(at, 128, stride=first_rows), :] = re[j * 128 : (j + 1) * 128]
            out_ref[pl.ds(at + 1, 128, stride=first_rows), :] = im[j * 128 : (j + 1) * 128]


def mask_kernel(place_ref, sampling_ref, out_ref):
    frames, full, cols = sampling_ref.shape
    groups = cols // 128
    lane = lax.broadcasted_iota(jnp.int32, (cols, cols), 1)
    freq = lax.broadcasted_iota(jnp.int32, (cols, cols), 0)
    wanted = (lane // 128) * 128 + place_ref[0]
    total = jnp.zeros((full, cols), f32)
    for f in range(frames):
        mine = (freq == wanted) & ((lane % 128) // (128 // frames) == f)
        chosen = jnp.where(mine, 1.0, 0.0).astype(bf16)
        total += mm(sampling_ref[f].astype(f32).astype(bf16), chosen, ((1,), (0,)))
    for j in range(groups):
        out_ref[j] = total[:, j * 128 : (j + 1) * 128]


def lanes(values):
    row = jnp.sum(values, axis=0, keepdims=True)
    return row[:, :128] + row[:, 128:256] + row[:, 256:384]


def smooth_kernel(place_ref, field_ref, before_ref, after_ref, residual_ref, out_ref, stats_ref):
    slab, slabs, frame, frames = (place_ref[i] for i in range(4))
    rows = residual_ref.shape[1]
    zdim, cols = residual_ref.shape[2:]
    nearer = jnp.maximum(frame - 1, 0)
    later = jnp.minimum(frame + 1, frames - 1)
    has_prev_frame = jnp.where(frame > 0, 1.0, 0.0)
    has_next_frame = jnp.where(frame < frames - 1, 1.0, 0.0)
    has_prev_row = jnp.where(slab > 0, 1.0, 0.0)
    has_next_row = jnp.where(slab < slabs - 1, 1.0, 0.0)
    zero_col = jnp.zeros((zdim, 1), f32)
    zero_slice = jnp.zeros((1, cols), f32)
    dots = jnp.zeros((1, 128), f32)
    norm = jnp.zeros((1, 128), f32)
    for r in range(rows):
        weight = field_ref[frame, 2, r]
        old_weight = field_ref[nearer, 2, r] * has_prev_frame
        now_weight = weight * has_next_frame
        for p in range(2):
            v = field_ref[frame, p, r]
            term = old_weight * (v - field_ref[nearer, p, r])
            term -= now_weight * (field_ref[later, p, r] - v)
            if r > 0:
                term += field_ref[frame, 2, r - 1] * (v - field_ref[frame, p, r - 1])
            else:
                term += before_ref[2] * has_prev_row * (v - before_ref[p])
            if r < rows - 1:
                term -= weight * (field_ref[frame, p, r + 1] - v)
            else:
                term -= weight * has_next_row * (after_ref[p] - v)
            flux = weight[:-1] * (v[1:] - v[:-1])
            term += jnp.concatenate([zero_slice, flux], axis=0)
            term -= jnp.concatenate([flux, zero_slice], axis=0)
            flux = weight[:, :-1] * (v[:, 1:] - v[:, :-1])
            term += jnp.concatenate([zero_col, flux], axis=1)
            term -= jnp.concatenate([flux, zero_col], axis=1)
            term = smooth_scale * term
            out_ref[p, r] = term
            dots += lanes(v * term)
            norm += lanes(residual_ref[p, r] * residual_ref[p, r])
    stats_ref[0:1, :] = dots
    stats_ref[1:2, :] = norm


def middle_kernel(in_ref, mask_ref, stats_ref, forward_ref, inverse_ref, out_ref):
    groups = mask_ref.shape[0]
    rows = 3
    forward = forward_ref[...]
    forward = jnp.concatenate([forward, forward], axis=1)
    inverse = inverse_ref[...]
    inverse = jnp.concatenate([inverse, inverse], axis=1)
    half = forward.shape[0] // 2
    energy = jnp.zeros((1, 128), f32)
    for j in range(groups):
        parts = []
        for r in range(rows):
            at = (j * rows + r) * 2
            re = in_ref[pl.ds(at, 128, stride=first_rows), :]
            im = in_ref[pl.ds(at + 1, 128, stride=first_rows), :]
            parts.append(jnp.concatenate([re, im], axis=1))
        upper, lower = split(jnp.concatenate(parts, axis=0))
        got = mm(forward, jnp.concatenate([upper, lower], axis=0), ((1,), (0,)))
        mask = mask_ref[j]
        re = (got[:half, :128] + got[half:, 128:]) * mask
        im = (got[:half, 128:] - got[half:, :128]) * mask
        energy += jnp.sum(re * re + im * im, axis=0, keepdims=True)
        upper, lower = split(jnp.concatenate([re, im], axis=1))
        got = mm(inverse, jnp.concatenate([upper, lower], axis=0), ((1,), (0,)))
        re = got[:half, :128] - got[half:, 128:]
        im = got[:half, 128:] + got[half:, :128]
        for r in range(rows):
            at = (r * groups + j) * 2
            out_ref[pl.ds(at, 128, stride=second_rows), :] = re[r * 128 : (r + 1) * 128]
            out_ref[pl.ds(at + 1, 128, stride=second_rows), :] = im[r * 128 : (r + 1) * 128]
    energy = energy + stats_ref[0:1, :]
    out_ref[pl.ds(first_rows, 128, stride=second_rows), :] = jnp.broadcast_to(energy, (128, 128))
    out_ref[pl.ds(first_rows + 1, 128, stride=second_rows), :] = jnp.broadcast_to(
        stats_ref[1:2, :], (128, 128)
    )


def combine_kernel(in_ref, sens_ref, table_ref, out_ref):
    coils, rows, zdim, cols = sens_ref.shape[1:]
    frames = out_ref.shape[0]
    table = table_ref[...]
    table = jnp.concatenate([table, table], axis=0)
    groups = cols // 128
    span = coils * zdim
    for r in range(rows):
        real, imag = [], []
        for j in range(groups):
            at = (r * groups + j) * 2
            real.append(in_ref[pl.ds(at, 128, stride=second_rows), :].T)
            imag.append(in_ref[pl.ds(at + 1, 128, stride=second_rows), :].T)
        both = jnp.concatenate(
            [jnp.concatenate(real, axis=1), jnp.concatenate(imag, axis=1)], axis=0
        )
        upper, lower = split(both)
        got = mm(jnp.concatenate([upper, lower], axis=1), table, ((1,), (0,)))
        re = got[:128, :cols] - got[128:, cols:]
        im = got[128:, :cols] + got[:128, cols:]
        s_re = sens_rows(sens_ref, 0, r, coils)
        s_im = sens_rows(sens_ref, 1, r, coils)
        for f in range(frames):
            b_re = re[f * span : (f + 1) * span]
            b_im = im[f * span : (f + 1) * span]
            for p, t in enumerate((s_re * b_re + s_im * b_im, s_re * b_im - s_im * b_re)):
                eight = t[0:8]
                for g in range(1, span // 8):
                    eight = eight + t[g * 8 : (g + 1) * 8]
                out_ref[f, p * rows + r] = eight[0:zdim] + eight[zdim : 2 * zdim]
    energy = jnp.sum(in_ref[pl.ds(first_rows, 128, stride=second_rows), :], axis=0, keepdims=True)
    norm = jnp.sum(in_ref[pl.ds(first_rows + 1, 128, stride=second_rows), :], axis=0, keepdims=True)
    filler = jnp.zeros((1, cols - 256), f32)
    line = jnp.concatenate([energy, norm, filler], axis=1)
    plane = jnp.concatenate([line, jnp.zeros((zdim - 1, cols), f32)], axis=0)
    for f in range(frames):
        out_ref[f, 2 * rows] = plane


def step_kernel(
    sums_ref, smooth_ref, iterate_ref, residual_ref, direction_ref, new_iterate_ref, new_residual_ref, norms_ref, old_ref
):
    planes = residual_ref.shape[0]
    sources = sums_ref.shape[0]
    line = sums_ref[0, planes][0:1]
    for i in range(1, sources):
        line = line + sums_ref[i, planes][0:1]
    curvature = jnp.sum(line[:, :128], axis=1, keepdims=True)
    old_norm = jnp.sum(line[:, 128:256], axis=1, keepdims=True)
    step = old_norm / curvature
    norm = jnp.zeros((1, 128), f32)
    for i in range(planes):
        applied = smooth_ref[i]
        for k in range(sources):
            applied = applied + sums_ref[k, i]
        new_iterate_ref[i] = iterate_ref[i] + step * direction_ref[i]
        fresh = residual_ref[i] - step * applied
        new_residual_ref[i] = fresh
        norm = norm + lanes(fresh * fresh)
    norms_ref[...] = jnp.broadcast_to(norm[None], norms_ref.shape)
    old_ref[...] = jnp.broadcast_to(old_norm, old_ref.shape)


def finish_kernel(norms_ref, old_ref, new_residual_ref, direction_ref, new_direction_ref, norm_ref):
    row = jnp.sum(norms_ref[...], axis=0)
    new_norm = jnp.sum(row, axis=1, keepdims=True)
    ratio = new_norm / old_ref[0:1, 0:1]
    for i in range(direction_ref.shape[0]):
        new_direction_ref[i] = new_residual_ref[i] + ratio * direction_ref[i]
    norm_ref[...] = jnp.broadcast_to(new_norm, norm_ref.shape)


vmem = pl.BlockSpec(memory_space=pltpu.VMEM)
smem = pl.BlockSpec(memory_space=pltpu.SMEM)


def call(kernel, ins, outs, name, scalars=0):
    shapes = [jax.ShapeDtypeStruct(s, f32) for s in outs]
    return pl.pallas_call(
        kernel,
        out_shape=shapes,
        in_specs=[smem] * scalars + [vmem] * (len(ins) - scalars),
        out_specs=[vmem] * len(outs),
        compiler_params=pltpu.CompilerParams(vmem_limit_bytes=40 * 1024 * 1024),
        name=name,
    )(*ins)


def swap(values, axis):
    pairs = values.reshape(values.shape[0] // 2, 2, 128)
    return lax.all_to_all(pairs, axis, 0, 0, tiled=True).reshape(values.shape)


def body(iterate, residual, direction, sensitivity, sampling, edge_weight):
    slabs = lax.axis_size(slab_axes)
    frames = lax.axis_size("coil")
    slab = lax.axis_index(slab_axes)
    frame = lax.axis_index("coil")
    rows, zdim, cols = direction.shape[3], direction.shape[2], direction.shape[4]

    sens = jnp.swapaxes(sensitivity, 2, 3)
    d = jnp.swapaxes(direction, 2, 3)[:, 0]
    r = jnp.swapaxes(residual, 2, 3)[:, 0]
    x = jnp.swapaxes(iterate, 2, 3)[:, 0]
    w = jnp.swapaxes(edge_weight, 1, 2).astype(f32)
    field = jnp.concatenate([d, w], axis=0)

    cos, sin = dft_tables(cols)
    by_slab = np.arange(cols).reshape(cols // rows, rows).T.reshape(-1)
    natural = jnp.asarray(np.concatenate([cos, sin], axis=0))
    forward = jnp.asarray(np.concatenate([cos[:, by_slab], sin[:, by_slab]], axis=0))
    inverse = jnp.asarray(np.concatenate([cos[by_slab], sin[by_slab]], axis=0))
    wide = jnp.asarray(np.concatenate([cos, sin], axis=1))

    place = jnp.stack([slab, jnp.int32(slabs), frame, jnp.int32(frames)]).astype(jnp.int32)
    fields = lax.all_gather(field, "coil", axis=0)
    up = [(i, i + 1) for i in range(slabs - 1)]
    before = lax.ppermute(field[:, rows - 1], slab_axes, up)
    after = lax.ppermute(field[:2, 0], slab_axes, [(j, i) for i, j in up])

    lines = slabs * first_rows
    (spectrum,) = call(images_kernel, (sens, fields, natural), [(lines, 128)], "images")
    spectrum = swap(spectrum, slab_axes)
    (mask,) = call(mask_kernel, (place, sampling), [(cols // 128, cols, 128)], "mask", 1)
    smooth, stats = call(
        smooth_kernel, (place, fields, before, after, r), [d.shape, (2, 128)], "smooth", 1
    )
    lines = slabs * second_rows
    (back,) = call(
        middle_kernel, (spectrum, mask, stats, forward, inverse), [(lines, 128)], "middle"
    )
    back = swap(back, slab_axes)
    (sums,) = call(
        combine_kernel, (back, sens, wide), [(frames, 2 * rows + 1, zdim, cols)], "combine"
    )
    sums = lax.all_to_all(sums, "coil", 0, 0, tiled=True)

    flat = (2 * rows, zdim, cols)
    near, far = ("y", "core"), ("z", "coil")
    new_x, new_r, norms, old = call(
        step_kernel,
        (sums, smooth.reshape(flat), x.reshape(flat), r.reshape(flat), d.reshape(flat)),
        [flat, flat, (lax.axis_size(near), 1, 128), (1, 128)],
        "step",
    )
    norms = lax.all_to_all(norms, near, 0, 0, tiled=True)
    norms = jnp.broadcast_to(
        jnp.sum(norms, axis=0, keepdims=True), (lax.axis_size(far), 1, 128)
    )
    norms = lax.all_to_all(norms, far, 0, 0, tiled=True)
    new_d, norm = call(
        finish_kernel, (norms, old, new_r, d.reshape(flat)), [flat, (1, 128)], "finish"
    )

    def restore(values):
        return jnp.swapaxes(values.reshape(2, 1, rows, zdim, cols), 2, 3)

    return restore(new_x), restore(new_r), restore(new_d), norm[0, 0]


def solution(mesh):
    fine = Mesh(mesh.devices.reshape(8, 8, 2, 4), ("z", "y", "core", "coil"))
    image = P(None, "coil", None, slab_axes, None)
    return jax.shard_map(
        body,
        mesh=fine,
        in_specs=(image, image, image, image, P(), P("coil", None, slab_axes, None)),
        out_specs=(image, image, image, P()),
        check_vma=False,
    )
```

```python
import functools
import math

import jax
import jax.numpy as jnp
import ml_dtypes
import numpy as np
from jax import lax
from jax.experimental import pallas as pl
from jax.experimental.pallas import tpu as pltpu
from jax.sharding import Mesh
from jax.sharding import PartitionSpec as P

smooth_scale = 0.05
slab_axes = ("z", "y", "core")
f32 = jnp.float32
bf16 = jnp.bfloat16

extra = 18
message = 19


def dft_tables(length):
    counter = np.arange(length, dtype=np.int64)
    phases = (counter[:, None] * counter[None, :]) % length
    angles = phases.astype(np.float32) * np.float32(2.0 * math.pi / length)
    unit_norm = np.float32(1.0 / math.sqrt(length))
    wide = angles.astype(np.float64)
    cos = np.cos(wide).astype(np.float32) * unit_norm
    sin = np.sin(wide).astype(np.float32) * unit_norm
    return cos.astype(ml_dtypes.bfloat16), sin.astype(ml_dtypes.bfloat16)


def split(values):
    upper = values.astype(bf16)
    return upper, (values - upper.astype(f32)).astype(bf16)


def mm(a, b, contract):
    return lax.dot_general(a, b, (contract, ((), ())), preferred_element_type=f32)


def sens_rows(sens_ref, part, row, coils):
    pieces = [sens_ref[part, c, row].astype(f32) for c in range(coils)]
    return jnp.concatenate(pieces, axis=0)


def images_kernel(sens_ref, all_ref, own_ref, weight_ref, table_ref, out_ref):
    coils, rows, zdim = sens_ref.shape[1:4]
    frames = all_ref.shape[1]
    table = table_ref[...]
    table = jnp.concatenate([table, table], axis=1)
    half = table.shape[0] // 2
    groups = half // 128
    for r in range(rows):
        s_re = sens_rows(sens_ref, 0, r, coils)
        s_im = sens_rows(sens_ref, 1, r, coils)
        real, imag = [], []
        for f in range(frames):
            d_re = jnp.concatenate([all_ref[0, f, r]] * coils, axis=0)
            d_im = jnp.concatenate([all_ref[1, f, r]] * coils, axis=0)
            real.append(s_re * d_re - s_im * d_im)
            imag.append(s_re * d_im + s_im * d_re)
        upper, lower = split(jnp.concatenate(real + imag, axis=0))
        got = mm(table, jnp.concatenate([upper, lower], axis=1), ((1,), (1,)))
        re = got[:half, :128] + got[half:, 128:]
        im = got[:half, 128:] - got[half:, :128]
        for j in range(groups):
            at = (j * rows + r) * 2
            out_ref[pl.ds(at, 128, stride=message), :] = re[j * 128 : (j + 1) * 128]
            out_ref[pl.ds(at + 1, 128, stride=message), :] = im[j * 128 : (j + 1) * 128]
    pieces = []
    for r in range(rows):
        for values in (own_ref[0, r], own_ref[1, r], weight_ref[r].astype(f32)):
            pieces += [values[:, j * 128 : (j + 1) * 128] for j in range(groups)]
    pieces.append(jnp.zeros((128 - len(pieces) * zdim, 128), f32))
    out_ref[pl.ds(extra, 128, stride=message), :] = jnp.concatenate(pieces, axis=0).T


def mask_kernel(place_ref, sampling_ref, out_ref):
    frames, full, cols = sampling_ref.shape
    groups = cols // 128
    lane = lax.broadcasted_iota(jnp.int32, (cols, cols), 1)
    freq = lax.broadcasted_iota(jnp.int32, (cols, cols), 0)
    wanted = (lane // 128) * 128 + place_ref[0]
    total = jnp.zeros((full, cols), f32)
    for f in range(frames):
        mine = (freq == wanted) & ((lane % 128) // (128 // frames) == f)
        chosen = jnp.where(mine, 1.0, 0.0).astype(bf16)
        total += mm(sampling_ref[f].astype(f32).astype(bf16), chosen, ((1,), (0,)))
    for j in range(groups):
        out_ref[j] = total[:, j * 128 : (j + 1) * 128]


def lanes(values):
    row = jnp.sum(values, axis=0, keepdims=True)
    return row[:, :128] + row[:, 128:256] + row[:, 256:384]


def smooth_kernel(place_ref, all_ref, own_ref, weight_ref, residual_ref, out_ref, next_ref, stats_ref):
    frame, frames = place_ref[1], place_ref[2]
    rows, zdim, cols = own_ref.shape[1:]
    later = jnp.minimum(frame + 1, frames - 1)
    zero_col = jnp.zeros((zdim, 1), f32)
    zero_slice = jnp.zeros((1, cols), f32)
    dots = jnp.zeros((1, 128), f32)
    norm = jnp.zeros((1, 128), f32)
    for r in range(rows):
        weight = weight_ref[r].astype(f32)
        for p in range(2):
            v = own_ref[p, r]
            rise = all_ref[p, later, r] - v
            onward = smooth_scale * (weight * rise)
            flux = weight[:-1] * (v[1:] - v[:-1])
            term = jnp.concatenate([zero_slice, flux], axis=0)
            term -= jnp.concatenate([flux, zero_slice], axis=0)
            flux = weight[:, :-1] * (v[:, 1:] - v[:, :-1])
            term += jnp.concatenate([zero_col, flux], axis=1)
            term -= jnp.concatenate([flux, zero_col], axis=1)
            term = smooth_scale * term
            out_ref[p * rows + r] = term - onward
            next_ref[p * rows + r] = onward
            dots += lanes(v * term + onward * rise)
            norm += lanes(residual_ref[p, r] * residual_ref[p, r])
    stats_ref[0:1, :] = dots
    stats_ref[1:2, :] = norm


def row_smoothing(given, zdim, groups):
    span = groups * zdim
    v, weight = [], []
    for r in range(3):
        at = r * 3 * span
        w = given[:, at + 2 * span : at + 3 * span]
        v.append(given[:, at : at + 2 * span])
        weight.append(jnp.concatenate([w, w], axis=1))
    none = jnp.zeros((1, 2 * span), f32)
    first = weight[0] * (v[1] - v[0])
    second = weight[1] * (v[2] - v[1])
    third = weight[2][:-1] * (v[0][1:] - v[2][:-1])
    terms = [
        jnp.concatenate([none, third], axis=0) - first,
        first - second,
        second - jnp.concatenate([third, none], axis=0),
    ]
    terms = [smooth_scale * t for t in terms]
    dots = v[0] * terms[0] + v[1] * terms[1] + v[2] * terms[2]
    return terms, jnp.sum(jnp.sum(dots, axis=0, keepdims=True), axis=1, keepdims=True)


def middle_kernel(in_ref, mask_ref, stats_ref, forward_ref, inverse_ref, out_ref, *, zdim):
    groups = mask_ref.shape[0]
    rows = 3
    forward = forward_ref[...]
    forward = jnp.concatenate([forward, forward], axis=1)
    inverse = inverse_ref[...]
    inverse = jnp.concatenate([inverse, inverse], axis=1)
    half = forward.shape[0] // 2
    energy = stats_ref[0:1, :]
    for j in range(groups):
        parts = []
        for r in range(rows):
            at = (j * rows + r) * 2
            re = in_ref[pl.ds(at, 128, stride=message), :]
            im = in_ref[pl.ds(at + 1, 128, stride=message), :]
            parts.append(jnp.concatenate([re, im], axis=1))
        upper, lower = split(jnp.concatenate(parts, axis=0))
        got = mm(forward, jnp.concatenate([upper, lower], axis=0), ((1,), (0,)))
        mask = mask_ref[j]
        re = (got[:half, :128] + got[half:, 128:]) * mask
        im = (got[:half, 128:] - got[half:, :128]) * mask
        energy += jnp.sum(re * re + im * im, axis=0, keepdims=True)
        upper, lower = split(jnp.concatenate([re, im], axis=1))
        got = mm(inverse, jnp.concatenate([upper, lower], axis=0), ((1,), (0,)))
        re = got[:half, :128] - got[half:, 128:]
        im = got[:half, 128:] + got[half:, :128]
        for r in range(rows):
            at = (r * groups + j) * 2
            out_ref[pl.ds(at, 128, stride=message), :] = re[r * 128 : (r + 1) * 128]
            out_ref[pl.ds(at + 1, 128, stride=message), :] = im[r * 128 : (r + 1) * 128]
    terms, dots = row_smoothing(in_ref[pl.ds(extra, 128, stride=message), :], zdim, groups)
    energy = jnp.sum(energy, axis=1, keepdims=True) + dots
    norm = jnp.sum(stats_ref[1:2, :], axis=1, keepdims=True)
    used = 2 * rows * groups * zdim
    filler = jnp.zeros((128, 128 - used - 2), f32)
    sums = [jnp.broadcast_to(v, (128, 1)) for v in (energy, norm)]
    out_ref[pl.ds(extra, 128, stride=message), :] = jnp.concatenate(terms + sums + [filler], axis=1)


def combine_kernel(place_ref, in_ref, sens_ref, smooth_ref, next_ref, table_ref, out_ref):
    frame, frame_count = place_ref[1], place_ref[2]
    coils, rows, zdim, cols = sens_ref.shape[1:]
    frames = out_ref.shape[0]
    table = table_ref[...]
    table = jnp.concatenate([table, table], axis=0)
    groups = cols // 128
    span = coils * zdim
    for r in range(rows):
        real, imag = [], []
        for j in range(groups):
            at = (r * groups + j) * 2
            real.append(in_ref[pl.ds(at, 128, stride=message), :].T)
            imag.append(in_ref[pl.ds(at + 1, 128, stride=message), :].T)
        both = jnp.concatenate(
            [jnp.concatenate(real, axis=1), jnp.concatenate(imag, axis=1)], axis=0
        )
        upper, lower = split(both)
        got = mm(jnp.concatenate([upper, lower], axis=1), table, ((1,), (0,)))
        re = got[:128, :cols] - got[128:, cols:]
        im = got[128:, :cols] + got[:128, cols:]
        s_re = sens_rows(sens_ref, 0, r, coils)
        s_im = sens_rows(sens_ref, 1, r, coils)
        for f in range(frames):
            b_re = re[f * span : (f + 1) * span]
            b_im = im[f * span : (f + 1) * span]
            for p, t in enumerate((s_re * b_re + s_im * b_im, s_re * b_im - s_im * b_re)):
                eight = t[0:8]
                for g in range(1, span // 8):
                    eight = eight + t[g * 8 : (g + 1) * 8]
                out_ref[f, p * rows + r] = eight[0:zdim] + eight[zdim : 2 * zdim]
    given = in_ref[pl.ds(extra, 128, stride=message), :]
    used = 2 * rows * groups * zdim
    total = jnp.sum(given, axis=0, keepdims=True)
    energy = jnp.broadcast_to(total[:, used : used + 1], (1, cols))
    norm = jnp.broadcast_to(total[:, used + 1 : used + 2], (1, cols))
    plane = jnp.concatenate([energy, norm, jnp.zeros((zdim - 2, cols), f32)], axis=0)
    for f in range(frames):
        out_ref[f, 2 * rows] = plane
    turned = given.T
    for r in range(rows):
        for p in range(2):
            at = (r * 2 + p) * groups * zdim
            term = [turned[at + j * zdim : at + (j + 1) * zdim] for j in range(groups)]
            i = p * rows + r
            out_ref[frame, i] += smooth_ref[i] + jnp.concatenate(term, axis=1)

    @pl.when(frame < frame_count - 1)
    def _():
        for i in range(2 * rows):
            out_ref[frame + 1, i] += next_ref[i]


def step_kernel(
    sums_ref, iterate_ref, residual_ref, direction_ref, new_iterate_ref, new_residual_ref, norms_ref, old_ref
):
    planes = residual_ref.shape[0]
    sources = sums_ref.shape[0]

    def total(i):
        value = sums_ref[0, i]
        for k in range(1, sources):
            value = value + sums_ref[k, i]
        return value

    both = total(planes)
    old_norm = both[1:2, :1]
    step = old_norm / both[0:1, :1]
    norm = jnp.zeros((1, 128), f32)
    for i in range(planes):
        new_iterate_ref[i] = iterate_ref[i] + step * direction_ref[i]
        fresh = residual_ref[i] - step * total(i)
        new_residual_ref[i] = fresh
        norm = norm + lanes(fresh * fresh)
    norms_ref[...] = jnp.broadcast_to(norm[None], norms_ref.shape)
    old_ref[...] = jnp.broadcast_to(old_norm, old_ref.shape)


def finish_kernel(norms_ref, old_ref, new_residual_ref, direction_ref, new_direction_ref, norm_ref):
    row = jnp.sum(norms_ref[...], axis=0)
    new_norm = jnp.sum(row, axis=1, keepdims=True)
    ratio = new_norm / old_ref[0:1, 0:1]
    for i in range(direction_ref.shape[0]):
        new_direction_ref[i] = new_residual_ref[i] + ratio * direction_ref[i]
    norm_ref[...] = jnp.broadcast_to(new_norm, norm_ref.shape)


vmem = pl.BlockSpec(memory_space=pltpu.VMEM)
smem = pl.BlockSpec(memory_space=pltpu.SMEM)


def call(kernel, ins, outs, name, scalars=0):
    shapes = [jax.ShapeDtypeStruct(s, f32) for s in outs]
    return pl.pallas_call(
        kernel,
        out_shape=shapes,
        in_specs=[smem] * scalars + [vmem] * (len(ins) - scalars),
        out_specs=[vmem] * len(outs),
        compiler_params=pltpu.CompilerParams(vmem_limit_bytes=40 * 1024 * 1024),
        name=name,
    )(*ins)


def swap(values, axis):
    single = values.reshape(values.shape[0], 1, 128)
    return lax.all_to_all(single, axis, 0, 0, tiled=True).reshape(values.shape)


def body(iterate, residual, direction, sensitivity, sampling, edge_weight):
    slabs = lax.axis_size(slab_axes)
    frames = lax.axis_size("coil")
    rows, zdim, cols = direction.shape[3], direction.shape[2], direction.shape[4]

    sens = jnp.swapaxes(sensitivity, 2, 3)
    d = jnp.swapaxes(direction, 2, 3)[:, 0]
    r = jnp.swapaxes(residual, 2, 3)[:, 0]
    x = jnp.swapaxes(iterate, 2, 3)[:, 0]
    w = jnp.swapaxes(edge_weight, 1, 2)[0]

    cos, sin = dft_tables(cols)
    by_slab = np.arange(cols).reshape(cols // rows, rows).T.reshape(-1)
    natural = jnp.asarray(np.concatenate([cos, sin], axis=0))
    forward = jnp.asarray(np.concatenate([cos[:, by_slab], sin[:, by_slab]], axis=0))
    inverse = jnp.asarray(np.concatenate([cos[by_slab], sin[by_slab]], axis=0))
    wide = jnp.asarray(np.concatenate([cos, sin], axis=1))

    place = jnp.stack([lax.axis_index(slab_axes), lax.axis_index("coil"), jnp.int32(frames)])
    place = place.astype(jnp.int32)
    gathered = lax.all_gather(direction, "coil", axis=1, tiled=True)
    gathered = jnp.swapaxes(gathered, 2, 3)

    lines = slabs * message
    (spectrum,) = call(images_kernel, (sens, gathered, d, w, natural), [(lines, 128)], "images")
    spectrum = swap(spectrum, slab_axes)
    (mask,) = call(mask_kernel, (place, sampling), [(cols // 128, cols, 128)], "mask", 1)
    flat = (2 * rows, zdim, cols)
    smooth, onward, stats = call(
        smooth_kernel, (place, gathered, d, w, r), [flat, flat, (2, 128)], "smooth", 1
    )
    (back,) = call(
        functools.partial(middle_kernel, zdim=zdim),
        (spectrum, mask, stats, forward, inverse),
        [(lines, 128)],
        "middle",
    )
    back = swap(back, slab_axes)
    (sums,) = call(
        combine_kernel,
        (place, back, sens, smooth, onward, wide),
        [(frames, 2 * rows + 1, zdim, cols)],
        "combine",
        1,
    )
    sums = lax.all_to_all(sums, "coil", 0, 0, tiled=True)

    near, far = ("y", "core"), ("z", "coil")
    new_x, new_r, norms, old = call(
        step_kernel,
        (sums, x.reshape(flat), r.reshape(flat), d.reshape(flat)),
        [flat, flat, (lax.axis_size(near), 1, 128), (1, 128)],
        "step",
    )
    norms = lax.all_to_all(norms, near, 0, 0, tiled=True)
    norms = jnp.broadcast_to(
        jnp.sum(norms, axis=0, keepdims=True), (lax.axis_size(far), 1, 128)
    )
    norms = lax.all_to_all(norms, far, 0, 0, tiled=True)
    new_d, norm = call(
        finish_kernel, (norms, old, new_r, d.reshape(flat)), [flat, (1, 128)], "finish"
    )

    def restore(values):
        return jnp.swapaxes(values.reshape(2, 1, rows, zdim, cols), 2, 3)

    return restore(new_x), restore(new_r), restore(new_d), norm[0, 0]


def solution(mesh):
    fine = Mesh(mesh.devices.reshape(8, 8, 2, 4), ("z", "y", "core", "coil"))
    image = P(None, "coil", None, slab_axes, None)
    return jax.shard_map(
        body,
        mesh=fine,
        in_specs=(image, image, image, image, P(), P("coil", None, slab_axes, None)),
        out_specs=(image, image, image, P()),
        check_vma=False,
    )
```

```python
import functools
import math

import jax
import jax.numpy as jnp
import ml_dtypes
import numpy as np
from jax import lax
from jax.experimental import pallas as pl
from jax.experimental.pallas import tpu as pltpu
from jax.sharding import Mesh
from jax.sharding import PartitionSpec as P

smooth_scale = 0.05
slab_axes = ("z", "y", "core")
f32 = jnp.float32
bf16 = jnp.bfloat16

extra = 18
message = 19


def dft_tables(length):
    counter = np.arange(length, dtype=np.int64)
    phases = (counter[:, None] * counter[None, :]) % length
    angles = phases.astype(np.float32) * np.float32(2.0 * math.pi / length)
    unit_norm = np.float32(1.0 / math.sqrt(length))
    wide = angles.astype(np.float64)
    cos = np.cos(wide).astype(np.float32) * unit_norm
    sin = np.sin(wide).astype(np.float32) * unit_norm
    return cos.astype(ml_dtypes.bfloat16), sin.astype(ml_dtypes.bfloat16)


def split(values):
    upper = values.astype(bf16)
    return upper, (values - upper.astype(f32)).astype(bf16)


def mm(a, b, contract):
    return lax.dot_general(a, b, (contract, ((), ())), preferred_element_type=f32)


def sens_rows(sens_ref, part, row, coils):
    pieces = [sens_ref[part, c, row].astype(f32) for c in range(coils)]
    return jnp.concatenate(pieces, axis=0)


def fetch_kernel(field_ref, *refs):
    count = (len(refs) - 2) // 2
    sources, copies_ref, held, done = refs[:count], refs[count], refs[count + 1 : -1], refs[-1]
    copies = [(sources[i], held[i]) for i in range(count)]
    copies += [(field_ref, copies_ref.at[i]) for i in range(copies_ref.shape[0])]
    copies = [pltpu.make_async_copy(a, b, done.at[i]) for i, (a, b) in enumerate(copies)]
    for copy in copies:
        copy.start()
    for copy in copies:
        copy.wait()


def images_kernel(all_ref, sens_ref, table_ref, own_ref, weight_ref, out_ref):
    coils, rows, zdim = sens_ref.shape[1:4]
    frames = all_ref.shape[0]
    table = table_ref[...]
    table = jnp.concatenate([table, table], axis=1)
    half = table.shape[0] // 2
    groups = half // 128
    for r in range(rows):
        s_re = sens_rows(sens_ref, 0, r, coils)
        s_im = sens_rows(sens_ref, 1, r, coils)
        real, imag = [], []
        for f in range(frames):
            d_re = jnp.concatenate([all_ref[f, 0, r]] * coils, axis=0)
            d_im = jnp.concatenate([all_ref[f, 1, r]] * coils, axis=0)
            real.append(s_re * d_re - s_im * d_im)
            imag.append(s_re * d_im + s_im * d_re)
        upper, lower = split(jnp.concatenate(real + imag, axis=0))
        got = mm(table, jnp.concatenate([upper, lower], axis=1), ((1,), (1,)))
        re = got[:half, :128] + got[half:, 128:]
        im = got[:half, 128:] - got[half:, :128]
        for j in range(groups):
            at = (j * rows + r) * 2
            out_ref[pl.ds(at, 128, stride=message), :] = re[j * 128 : (j + 1) * 128]
            out_ref[pl.ds(at + 1, 128, stride=message), :] = im[j * 128 : (j + 1) * 128]
    pieces = []
    for r in range(rows):
        for values in (own_ref[0, r], own_ref[1, r], weight_ref[r].astype(f32)):
            pieces += [values[:, j * 128 : (j + 1) * 128] for j in range(groups)]
    pieces.append(jnp.zeros((128 - len(pieces) * zdim, 128), f32))
    out_ref[pl.ds(extra, 128, stride=message), :] = jnp.concatenate(pieces, axis=0).T


def mask_kernel(place_ref, sampling_ref, out_ref):
    frames, full, cols = sampling_ref.shape
    groups = cols // 128
    lane = lax.broadcasted_iota(jnp.int32, (cols, cols), 1)
    freq = lax.broadcasted_iota(jnp.int32, (cols, cols), 0)
    wanted = (lane // 128) * 128 + place_ref[0]
    total = jnp.zeros((full, cols), f32)
    for f in range(frames):
        mine = (freq == wanted) & ((lane % 128) // (128 // frames) == f)
        chosen = jnp.where(mine, 1.0, 0.0).astype(bf16)
        total += mm(sampling_ref[f].astype(f32).astype(bf16), chosen, ((1,), (0,)))
    for j in range(groups):
        out_ref[j] = total[:, j * 128 : (j + 1) * 128]


def lanes(values):
    row = jnp.sum(values, axis=0, keepdims=True)
    return row[:, :128] + row[:, 128:256] + row[:, 256:384]


def smooth_kernel(place_ref, all_ref, own_ref, weight_ref, residual_ref, out_ref, next_ref, stats_ref):
    frame, frames = place_ref[1], place_ref[2]
    rows, zdim, cols = own_ref.shape[1:]
    later = jnp.minimum(frame + 1, frames - 1)
    zero_col = jnp.zeros((zdim, 1), f32)
    zero_slice = jnp.zeros((1, cols), f32)
    dots = jnp.zeros((1, 128), f32)
    norm = jnp.zeros((1, 128), f32)
    for r in range(rows):
        weight = weight_ref[r].astype(f32)
        for p in range(2):
            v = own_ref[p, r]
            rise = all_ref[later, p, r] - v
            onward = smooth_scale * (weight * rise)
            flux = weight[:-1] * (v[1:] - v[:-1])
            term = jnp.concatenate([zero_slice, flux], axis=0)
            term -= jnp.concatenate([flux, zero_slice], axis=0)
            flux = weight[:, :-1] * (v[:, 1:] - v[:, :-1])
            term += jnp.concatenate([zero_col, flux], axis=1)
            term -= jnp.concatenate([flux, zero_col], axis=1)
            term = smooth_scale * term
            out_ref[p * rows + r] = term - onward
            next_ref[p * rows + r] = onward
            dots += lanes(v * term + onward * rise)
            norm += lanes(residual_ref[p, r] * residual_ref[p, r])
    stats_ref[0:1, :] = dots
    stats_ref[1:2, :] = norm


def row_smoothing(given, zdim, groups):
    span = groups * zdim
    v, weight = [], []
    for r in range(3):
        at = r * 3 * span
        w = given[:, at + 2 * span : at + 3 * span]
        v.append(given[:, at : at + 2 * span])
        weight.append(jnp.concatenate([w, w], axis=1))
    none = jnp.zeros((1, 2 * span), f32)
    first = weight[0] * (v[1] - v[0])
    second = weight[1] * (v[2] - v[1])
    third = weight[2][:-1] * (v[0][1:] - v[2][:-1])
    terms = [
        jnp.concatenate([none, third], axis=0) - first,
        first - second,
        second - jnp.concatenate([third, none], axis=0),
    ]
    terms = [smooth_scale * t for t in terms]
    dots = v[0] * terms[0] + v[1] * terms[1] + v[2] * terms[2]
    return terms, jnp.sum(jnp.sum(dots, axis=0, keepdims=True), axis=1, keepdims=True)


def middle_kernel(in_ref, mask_ref, stats_ref, forward_ref, inverse_ref, out_ref, *, zdim):
    groups = mask_ref.shape[0]
    rows = 3
    forward = forward_ref[...]
    forward = jnp.concatenate([forward, forward], axis=1)
    inverse = inverse_ref[...]
    inverse = jnp.concatenate([inverse, inverse], axis=1)
    half = forward.shape[0] // 2
    energy = stats_ref[0:1, :]
    for j in range(groups):
        parts = []
        for r in range(rows):
            at = (j * rows + r) * 2
            re = in_ref[pl.ds(at, 128, stride=message), :]
            im = in_ref[pl.ds(at + 1, 128, stride=message), :]
            parts.append(jnp.concatenate([re, im], axis=1))
        upper, lower = split(jnp.concatenate(parts, axis=0))
        got = mm(forward, jnp.concatenate([upper, lower], axis=0), ((1,), (0,)))
        mask = mask_ref[j]
        re = (got[:half, :128] + got[half:, 128:]) * mask
        im = (got[:half, 128:] - got[half:, :128]) * mask
        energy += jnp.sum(re * re + im * im, axis=0, keepdims=True)
        upper, lower = split(jnp.concatenate([re, im], axis=1))
        got = mm(inverse, jnp.concatenate([upper, lower], axis=0), ((1,), (0,)))
        re = got[:half, :128] - got[half:, 128:]
        im = got[:half, 128:] + got[half:, :128]
        for r in range(rows):
            at = (r * groups + j) * 2
            out_ref[pl.ds(at, 128, stride=message), :] = re[r * 128 : (r + 1) * 128]
            out_ref[pl.ds(at + 1, 128, stride=message), :] = im[r * 128 : (r + 1) * 128]
    terms, dots = row_smoothing(in_ref[pl.ds(extra, 128, stride=message), :], zdim, groups)
    energy = jnp.sum(energy, axis=1, keepdims=True) + dots
    norm = jnp.sum(stats_ref[1:2, :], axis=1, keepdims=True)
    used = 2 * rows * groups * zdim
    filler = jnp.zeros((128, 128 - used - 2), f32)
    sums = [jnp.broadcast_to(v, (128, 1)) for v in (energy, norm)]
    out_ref[pl.ds(extra, 128, stride=message), :] = jnp.concatenate(terms + sums + [filler], axis=1)


def combine_kernel(place_ref, in_ref, sens_ref, smooth_ref, next_ref, table_ref, out_ref):
    frame, frame_count = place_ref[1], place_ref[2]
    coils, rows, zdim, cols = sens_ref.shape[1:]
    frames = out_ref.shape[0]
    table = table_ref[...]
    table = jnp.concatenate([table, table], axis=0)
    groups = cols // 128
    span = coils * zdim
    for r in range(rows):
        real, imag = [], []
        for j in range(groups):
            at = (r * groups + j) * 2
            real.append(in_ref[pl.ds(at, 128, stride=message), :].T)
            imag.append(in_ref[pl.ds(at + 1, 128, stride=message), :].T)
        both = jnp.concatenate(
            [jnp.concatenate(real, axis=1), jnp.concatenate(imag, axis=1)], axis=0
        )
        upper, lower = split(both)
        got = mm(jnp.concatenate([upper, lower], axis=1), table, ((1,), (0,)))
        re = got[:128, :cols] - got[128:, cols:]
        im = got[128:, :cols] + got[:128, cols:]
        s_re = sens_rows(sens_ref, 0, r, coils)
        s_im = sens_rows(sens_ref, 1, r, coils)
        for f in range(frames):
            b_re = re[f * span : (f + 1) * span]
            b_im = im[f * span : (f + 1) * span]
            for p, t in enumerate((s_re * b_re + s_im * b_im, s_re * b_im - s_im * b_re)):
                eight = t[0:8]
                for g in range(1, span // 8):
                    eight = eight + t[g * 8 : (g + 1) * 8]
                out_ref[f, p * rows + r] = eight[0:zdim] + eight[zdim : 2 * zdim]
    given = in_ref[pl.ds(extra, 128, stride=message), :]
    used = 2 * rows * groups * zdim
    total = jnp.sum(given, axis=0, keepdims=True)
    energy = jnp.broadcast_to(total[:, used : used + 1], (1, cols))
    norm = jnp.broadcast_to(total[:, used + 1 : used + 2], (1, cols))
    plane = jnp.concatenate([energy, norm, jnp.zeros((zdim - 2, cols), f32)], axis=0)
    for f in range(frames):
        out_ref[f, 2 * rows] = plane
    turned = given.T
    for r in range(rows):
        for p in range(2):
            at = (r * 2 + p) * groups * zdim
            term = [turned[at + j * zdim : at + (j + 1) * zdim] for j in range(groups)]
            i = p * rows + r
            out_ref[frame, i] += smooth_ref[i] + jnp.concatenate(term, axis=1)

    @pl.when(frame < frame_count - 1)
    def _():
        for i in range(2 * rows):
            out_ref[frame + 1, i] += next_ref[i]


def step_kernel(
    sums_ref, iterate_ref, residual_ref, direction_ref, new_iterate_ref, new_residual_ref, kept_ref, norms_ref, old_ref
):
    planes = residual_ref.shape[0]
    sources = sums_ref.shape[0]

    def total(i):
        value = sums_ref[0, i]
        for k in range(1, sources):
            value = value + sums_ref[k, i]
        return value

    both = total(planes)
    old_norm = both[1:2, :1]
    step = old_norm / both[0:1, :1]
    norm = jnp.zeros((1, 128), f32)
    for i in range(planes):
        new_iterate_ref[i] = iterate_ref[i] + step * direction_ref[i]
        fresh = residual_ref[i] - step * total(i)
        new_residual_ref[i] = fresh
        kept_ref[i] = fresh
        norm = norm + lanes(fresh * fresh)
    norms_ref[...] = jnp.broadcast_to(norm[None], norms_ref.shape)
    old_ref[...] = jnp.broadcast_to(old_norm, old_ref.shape)


def finish_kernel(norms_ref, old_ref, new_residual_ref, direction_ref, new_direction_ref, norm_ref):
    row = jnp.sum(norms_ref[...], axis=0)
    new_norm = jnp.sum(row, axis=1, keepdims=True)
    ratio = new_norm / old_ref[0:1, 0:1]
    for i in range(direction_ref.shape[0]):
        new_direction_ref[i] = new_residual_ref[i] + ratio * direction_ref[i]
    norm_ref[...] = jnp.broadcast_to(new_norm, norm_ref.shape)


vmem = pl.BlockSpec(memory_space=pltpu.VMEM)
smem = pl.BlockSpec(memory_space=pltpu.SMEM)
hbm = pl.BlockSpec(memory_space=pltpu.HBM)


params = pltpu.CompilerParams(vmem_limit_bytes=40 * 1024 * 1024)


def call(kernel, ins, outs, name, scalars=0):
    return pl.pallas_call(
        kernel,
        out_shape=[jax.ShapeDtypeStruct(s, f32) for s in outs],
        in_specs=[smem] * scalars + [vmem] * (len(ins) - scalars),
        out_specs=[vmem] * len(outs),
        compiler_params=params,
        name=name,
    )(*ins)


def fetch(field, copies, others):
    shapes = [((copies,) + field.shape, field.dtype)] + [(a.shape, a.dtype) for a in others]
    return pl.pallas_call(
        fetch_kernel,
        out_shape=[jax.ShapeDtypeStruct(*s) for s in shapes],
        in_specs=[hbm] * (1 + len(others)),
        out_specs=[vmem] * len(shapes),
        scratch_shapes=[pltpu.SemaphoreType.DMA((copies + len(others),))],
        compiler_params=params,
        name="fetch",
    )(field, *others)


def swap(values, axis):
    single = values.reshape(values.shape[0], 1, 128)
    return lax.all_to_all(single, axis, 0, 0, tiled=True).reshape(values.shape)


def body(iterate, residual, direction, sensitivity, sampling, edge_weight):
    slabs = lax.axis_size(slab_axes)
    frames = lax.axis_size("coil")
    rows, zdim, cols = direction.shape[3], direction.shape[2], direction.shape[4]

    sens = jnp.swapaxes(sensitivity, 2, 3)
    d = jnp.swapaxes(direction, 2, 3)[:, 0]
    r = jnp.swapaxes(residual, 2, 3)[:, 0]
    x = jnp.swapaxes(iterate, 2, 3)[:, 0]
    w = jnp.swapaxes(edge_weight, 1, 2)[0]

    cos, sin = dft_tables(cols)
    by_slab = np.arange(cols).reshape(cols // rows, rows).T.reshape(-1)
    natural = jnp.asarray(np.concatenate([cos, sin], axis=0))
    forward = jnp.asarray(np.concatenate([cos[:, by_slab], sin[:, by_slab]], axis=0))
    inverse = jnp.asarray(np.concatenate([cos[by_slab], sin[by_slab]], axis=0))
    wide = jnp.asarray(np.concatenate([cos, sin], axis=1))

    place = jnp.stack([lax.axis_index(slab_axes), lax.axis_index("coil"), jnp.int32(frames)])
    place = place.astype(jnp.int32)
    copies, *near_by = fetch(d, frames, (sens, natural, d, w))
    gathered = lax.all_to_all(copies, "coil", 0, 0, tiled=True)

    lines = slabs * message
    (spectrum,) = call(images_kernel, (gathered, *near_by), [(lines, 128)], "images")
    spectrum = swap(spectrum, slab_axes)
    (mask,) = call(mask_kernel, (place, sampling), [(cols // 128, cols, 128)], "mask", 1)
    flat = (2 * rows, zdim, cols)
    smooth, onward, stats = call(
        smooth_kernel, (place, gathered, d, w, r), [flat, flat, (2, 128)], "smooth", 1
    )
    (back,) = call(
        functools.partial(middle_kernel, zdim=zdim),
        (spectrum, mask, stats, forward, inverse),
        [(lines, 128)],
        "middle",
    )
    back = swap(back, slab_axes)
    (sums,) = call(
        combine_kernel,
        (place, back, sens, smooth, onward, wide),
        [(frames, 2 * rows + 1, zdim, cols)],
        "combine",
        1,
    )
    sums = lax.all_to_all(sums, "coil", 0, 0, tiled=True)

    near, far = ("y", "core"), ("z", "coil")
    new_x, new_r, kept, norms, old = call(
        step_kernel,
        (sums, x.reshape(flat), r.reshape(flat), d.reshape(flat)),
        [flat, flat, flat, (lax.axis_size(near), 1, 128), (1, 128)],
        "step",
    )
    norms = lax.all_to_all(norms, near, 0, 0, tiled=True)
    norms = jnp.broadcast_to(
        jnp.sum(norms, axis=0, keepdims=True), (lax.axis_size(far), 1, 128)
    )
    norms = lax.all_to_all(norms, far, 0, 0, tiled=True)
    new_d, norm = call(
        finish_kernel, (norms, old, kept, d.reshape(flat)), [flat, (1, 128)], "finish"
    )

    def restore(values):
        return jnp.swapaxes(values.reshape(2, 1, rows, zdim, cols), 2, 3)

    return restore(new_x), restore(new_r), restore(new_d), norm[0, 0]


def solution(mesh):
    fine = Mesh(mesh.devices.reshape(8, 8, 2, 4), ("z", "y", "core", "coil"))
    image = P(None, "coil", None, slab_axes, None)
    return jax.shard_map(
        body,
        mesh=fine,
        in_specs=(image, image, image, image, P(), P("coil", None, slab_axes, None)),
        out_specs=(image, image, image, P()),
        check_vma=False,
    )
```

```python
import functools
import math

import jax
import jax.numpy as jnp
import ml_dtypes
import numpy as np
from jax import lax
from jax.experimental import pallas as pl
from jax.experimental.pallas import tpu as pltpu
from jax.sharding import Mesh
from jax.sharding import PartitionSpec as P

smooth_scale = 0.05
slab_axes = ("z", "y", "core")
f32 = jnp.float32
bf16 = jnp.bfloat16

extra = 18
message = 19


def dft_tables(length):
    counter = np.arange(length, dtype=np.int64)
    phases = (counter[:, None] * counter[None, :]) % length
    angles = phases.astype(np.float32) * np.float32(2.0 * math.pi / length)
    unit_norm = np.float32(1.0 / math.sqrt(length))
    wide = angles.astype(np.float64)
    cos = np.cos(wide).astype(np.float32) * unit_norm
    sin = np.sin(wide).astype(np.float32) * unit_norm
    return cos.astype(ml_dtypes.bfloat16), sin.astype(ml_dtypes.bfloat16)


def split(values):
    upper = values.astype(bf16)
    return upper, (values - upper.astype(f32)).astype(bf16)


def mm(a, b, contract):
    return lax.dot_general(a, b, (contract, ((), ())), preferred_element_type=f32)


def sens_rows(sens_ref, part, row, coils):
    pieces = [sens_ref[part, c, row].astype(f32) for c in range(coils)]
    return jnp.concatenate(pieces, axis=0)


def prepare_kernel(sens_ref, table_ref, own_ref, weight_ref, sens_out_ref, table_out_ref, extra_ref):
    coils, rows, zdim = sens_ref.shape[1:4]
    for p in range(2):
        for r in range(rows):
            sens_out_ref[p, r] = sens_rows(sens_ref, p, r, coils)
    table_out_ref[...] = table_ref[...]
    groups = own_ref.shape[3] // 128
    pieces = []
    for r in range(rows):
        for values in (own_ref[0, r], own_ref[1, r], weight_ref[r].astype(f32)):
            pieces += [values[:, j * 128 : (j + 1) * 128] for j in range(groups)]
    pieces.append(jnp.zeros((128 - len(pieces) * zdim, 128), f32))
    extra_ref[...] = jnp.concatenate(pieces, axis=0).T


def images_kernel(all_ref, sens_ref, table_ref, extra_ref, out_ref):
    frames, _, rows, zdim, _ = all_ref.shape
    coils = sens_ref.shape[2] // zdim
    table = table_ref[...]
    table = jnp.concatenate([table, table], axis=1)
    half = table.shape[0] // 2
    groups = half // 128
    for r in range(rows):
        s_re, s_im = sens_ref[0, r], sens_ref[1, r]
        real, imag = [], []
        for f in range(frames):
            d_re = jnp.concatenate([all_ref[f, 0, r]] * coils, axis=0)
            d_im = jnp.concatenate([all_ref[f, 1, r]] * coils, axis=0)
            real.append(s_re * d_re - s_im * d_im)
            imag.append(s_re * d_im + s_im * d_re)
        upper, lower = split(jnp.concatenate(real + imag, axis=0))
        got = mm(table, jnp.concatenate([upper, lower], axis=1), ((1,), (1,)))
        re = got[:half, :128] + got[half:, 128:]
        im = got[:half, 128:] - got[half:, :128]
        for j in range(groups):
            at = (j * rows + r) * 2
            out_ref[pl.ds(at, 128, stride=message), :] = re[j * 128 : (j + 1) * 128]
            out_ref[pl.ds(at + 1, 128, stride=message), :] = im[j * 128 : (j + 1) * 128]
    out_ref[pl.ds(extra, 128, stride=message), :] = extra_ref[...]


def mask_kernel(place_ref, sampling_ref, out_ref):
    frames, full, cols = sampling_ref.shape
    groups = cols // 128
    lane = lax.broadcasted_iota(jnp.int32, (cols, cols), 1)
    freq = lax.broadcasted_iota(jnp.int32, (cols, cols), 0)
    wanted = (lane // 128) * 128 + place_ref[0]
    total = jnp.zeros((full, cols), f32)
    for f in range(frames):
        mine = (freq == wanted) & ((lane % 128) // (128 // frames) == f)
        chosen = jnp.where(mine, 1.0, 0.0).astype(bf16)
        total += mm(sampling_ref[f].astype(f32).astype(bf16), chosen, ((1,), (0,)))
    for j in range(groups):
        out_ref[j] = total[:, j * 128 : (j + 1) * 128]


def lanes(values):
    row = jnp.sum(values, axis=0, keepdims=True)
    return row[:, :128] + row[:, 128:256] + row[:, 256:384]


def smooth_kernel(place_ref, all_ref, own_ref, weight_ref, residual_ref, out_ref, next_ref, stats_ref):
    frame, frames = place_ref[1], place_ref[2]
    rows, zdim, cols = own_ref.shape[1:]
    later = jnp.minimum(frame + 1, frames - 1)
    zero_col = jnp.zeros((zdim, 1), f32)
    zero_slice = jnp.zeros((1, cols), f32)
    dots = jnp.zeros((1, 128), f32)
    norm = jnp.zeros((1, 128), f32)
    for r in range(rows):
        weight = weight_ref[r].astype(f32)
        for p in range(2):
            v = own_ref[p, r]
            rise = all_ref[later, p, r] - v
            onward = smooth_scale * (weight * rise)
            flux = weight[:-1] * (v[1:] - v[:-1])
            term = jnp.concatenate([zero_slice, flux], axis=0)
            term -= jnp.concatenate([flux, zero_slice], axis=0)
            flux = weight[:, :-1] * (v[:, 1:] - v[:, :-1])
            term += jnp.concatenate([zero_col, flux], axis=1)
            term -= jnp.concatenate([flux, zero_col], axis=1)
            term = smooth_scale * term
            out_ref[p * rows + r] = term - onward
            next_ref[p * rows + r] = onward
            dots += lanes(v * term + onward * rise)
            norm += lanes(residual_ref[p, r] * residual_ref[p, r])
    stats_ref[0:1, :] = dots
    stats_ref[1:2, :] = norm


def row_smoothing(given, zdim, groups):
    span = groups * zdim
    v, weight = [], []
    for r in range(3):
        at = r * 3 * span
        w = given[:, at + 2 * span : at + 3 * span]
        v.append(given[:, at : at + 2 * span])
        weight.append(jnp.concatenate([w, w], axis=1))
    none = jnp.zeros((1, 2 * span), f32)
    first = weight[0] * (v[1] - v[0])
    second = weight[1] * (v[2] - v[1])
    third = weight[2][:-1] * (v[0][1:] - v[2][:-1])
    terms = [
        jnp.concatenate([none, third], axis=0) - first,
        first - second,
        second - jnp.concatenate([third, none], axis=0),
    ]
    terms = [smooth_scale * t for t in terms]
    dots = v[0] * terms[0] + v[1] * terms[1] + v[2] * terms[2]
    return terms, jnp.sum(jnp.sum(dots, axis=0, keepdims=True), axis=1, keepdims=True)


def middle_kernel(in_ref, mask_ref, stats_ref, forward_ref, inverse_ref, out_ref, *, zdim):
    groups = mask_ref.shape[0]
    rows = 3
    forward = forward_ref[...]
    forward = jnp.concatenate([forward, forward], axis=1)
    inverse = inverse_ref[...]
    inverse = jnp.concatenate([inverse, inverse], axis=1)
    half = forward.shape[0] // 2
    energy = stats_ref[0:1, :]
    for j in range(groups):
        parts = []
        for r in range(rows):
            at = (j * rows + r) * 2
            re = in_ref[pl.ds(at, 128, stride=message), :]
            im = in_ref[pl.ds(at + 1, 128, stride=message), :]
            parts.append(jnp.concatenate([re, im], axis=1))
        upper, lower = split(jnp.concatenate(parts, axis=0))
        got = mm(forward, jnp.concatenate([upper, lower], axis=0), ((1,), (0,)))
        mask = mask_ref[j]
        re = (got[:half, :128] + got[half:, 128:]) * mask
        im = (got[:half, 128:] - got[half:, :128]) * mask
        energy += jnp.sum(re * re + im * im, axis=0, keepdims=True)
        upper, lower = split(jnp.concatenate([re, im], axis=1))
        got = mm(inverse, jnp.concatenate([upper, lower], axis=0), ((1,), (0,)))
        re = got[:half, :128] - got[half:, 128:]
        im = got[:half, 128:] + got[half:, :128]
        for r in range(rows):
            at = (r * groups + j) * 2
            out_ref[pl.ds(at, 128, stride=message), :] = re[r * 128 : (r + 1) * 128]
            out_ref[pl.ds(at + 1, 128, stride=message), :] = im[r * 128 : (r + 1) * 128]
    terms, dots = row_smoothing(in_ref[pl.ds(extra, 128, stride=message), :], zdim, groups)
    energy = jnp.sum(energy, axis=1, keepdims=True) + dots
    norm = jnp.sum(stats_ref[1:2, :], axis=1, keepdims=True)
    used = 2 * rows * groups * zdim
    filler = jnp.zeros((128, 128 - used - 2), f32)
    sums = [jnp.broadcast_to(v, (128, 1)) for v in (energy, norm)]
    out_ref[pl.ds(extra, 128, stride=message), :] = jnp.concatenate(terms + sums + [filler], axis=1)


def combine_kernel(place_ref, in_ref, sens_ref, smooth_ref, next_ref, table_ref, out_ref):
    frame, frame_count = place_ref[1], place_ref[2]
    frames, _, zdim, cols = out_ref.shape
    rows, span = sens_ref.shape[1:3]
    table = table_ref[...]
    table = jnp.concatenate([table, table], axis=0)
    groups = cols // 128
    for r in range(rows):
        real, imag = [], []
        for j in range(groups):
            at = (r * groups + j) * 2
            real.append(in_ref[pl.ds(at, 128, stride=message), :].T)
            imag.append(in_ref[pl.ds(at + 1, 128, stride=message), :].T)
        both = jnp.concatenate(
            [jnp.concatenate(real, axis=1), jnp.concatenate(imag, axis=1)], axis=0
        )
        upper, lower = split(both)
        got = mm(jnp.concatenate([upper, lower], axis=1), table, ((1,), (0,)))
        re = got[:128, :cols] - got[128:, cols:]
        im = got[128:, :cols] + got[:128, cols:]
        s_re, s_im = sens_ref[0, r], sens_ref[1, r]
        for f in range(frames):
            b_re = re[f * span : (f + 1) * span]
            b_im = im[f * span : (f + 1) * span]
            for p, t in enumerate((s_re * b_re + s_im * b_im, s_re * b_im - s_im * b_re)):
                eight = t[0:8]
                for g in range(1, span // 8):
                    eight = eight + t[g * 8 : (g + 1) * 8]
                out_ref[f, p * rows + r] = eight[0:zdim] + eight[zdim : 2 * zdim]
    given = in_ref[pl.ds(extra, 128, stride=message), :]
    used = 2 * rows * groups * zdim
    total = jnp.sum(given, axis=0, keepdims=True)
    energy = jnp.broadcast_to(total[:, used : used + 1], (1, cols))
    norm = jnp.broadcast_to(total[:, used + 1 : used + 2], (1, cols))
    plane = jnp.concatenate([energy, norm, jnp.zeros((zdim - 2, cols), f32)], axis=0)
    for f in range(frames):
        out_ref[f, 2 * rows] = plane
    turned = given.T
    for r in range(rows):
        for p in range(2):
            at = (r * 2 + p) * groups * zdim
            term = [turned[at + j * zdim : at + (j + 1) * zdim] for j in range(groups)]
            i = p * rows + r
            out_ref[frame, i] += smooth_ref[i] + jnp.concatenate(term, axis=1)

    @pl.when(frame < frame_count - 1)
    def _():
        for i in range(2 * rows):
            out_ref[frame + 1, i] += next_ref[i]


def step_kernel(
    sums_ref, iterate_ref, residual_ref, direction_ref, new_iterate_ref, new_residual_ref, kept_ref, norms_ref, old_ref
):
    planes = residual_ref.shape[0]
    sources = sums_ref.shape[0]

    def total(i):
        value = sums_ref[0, i]
        for k in range(1, sources):
            value = value + sums_ref[k, i]
        return value

    both = total(planes)
    old_norm = both[1:2, :1]
    step = old_norm / both[0:1, :1]
    norm = jnp.zeros((1, 128), f32)
    for i in range(planes):
        new_iterate_ref[i] = iterate_ref[i] + step * direction_ref[i]
        fresh = residual_ref[i] - step * total(i)
        new_residual_ref[i] = fresh
        kept_ref[i] = fresh
        norm = norm + lanes(fresh * fresh)
    norms_ref[...] = jnp.broadcast_to(norm[None], norms_ref.shape)
    old_ref[...] = jnp.broadcast_to(old_norm, old_ref.shape)


def finish_kernel(norms_ref, old_ref, new_residual_ref, direction_ref, new_direction_ref, norm_ref):
    row = jnp.sum(norms_ref[...], axis=0)
    new_norm = jnp.sum(row, axis=1, keepdims=True)
    ratio = new_norm / old_ref[0:1, 0:1]
    for i in range(direction_ref.shape[0]):
        new_direction_ref[i] = new_residual_ref[i] + ratio * direction_ref[i]
    norm_ref[...] = jnp.broadcast_to(new_norm, norm_ref.shape)


vmem = pl.BlockSpec(memory_space=pltpu.VMEM)
smem = pl.BlockSpec(memory_space=pltpu.SMEM)


params = pltpu.CompilerParams(vmem_limit_bytes=40 * 1024 * 1024)


def call(kernel, ins, outs, name, scalars=0):
    return pl.pallas_call(
        kernel,
        out_shape=[
            jax.ShapeDtypeStruct(s, f32) if isinstance(s, tuple) else jax.ShapeDtypeStruct(s.shape, s.dtype)
            for s in outs
        ],
        in_specs=[smem] * scalars + [vmem] * (len(ins) - scalars),
        out_specs=[vmem] * len(outs),
        compiler_params=params,
        name=name,
    )(*ins)


def swap(values, axis):
    single = values.reshape(values.shape[0], 1, 128)
    return lax.all_to_all(single, axis, 0, 0, tiled=True).reshape(values.shape)


def body(iterate, residual, direction, sensitivity, sampling, edge_weight):
    slabs = lax.axis_size(slab_axes)
    frames = lax.axis_size("coil")
    rows, zdim, cols = direction.shape[3], direction.shape[2], direction.shape[4]

    sens = jnp.swapaxes(sensitivity, 2, 3)
    d = jnp.swapaxes(direction, 2, 3)[:, 0]
    r = jnp.swapaxes(residual, 2, 3)[:, 0]
    x = jnp.swapaxes(iterate, 2, 3)[:, 0]
    w = jnp.swapaxes(edge_weight, 1, 2)[0]

    cos, sin = dft_tables(cols)
    by_slab = np.arange(cols).reshape(cols // rows, rows).T.reshape(-1)
    natural = jnp.asarray(np.concatenate([cos, sin], axis=0))
    forward = jnp.asarray(np.concatenate([cos[:, by_slab], sin[:, by_slab]], axis=0))
    inverse = jnp.asarray(np.concatenate([cos[by_slab], sin[by_slab]], axis=0))
    wide = jnp.asarray(np.concatenate([cos, sin], axis=1))

    place = jnp.stack([lax.axis_index(slab_axes), lax.axis_index("coil"), jnp.int32(frames)])
    place = place.astype(jnp.int32)
    copies = jnp.broadcast_to(d[None], (frames,) + d.shape)
    gathered = lax.all_to_all(copies, "coil", 0, 0, tiled=True)
    sens_shape = (2, rows, sens.shape[1] * zdim, cols)
    sens, natural, extras = call(
        prepare_kernel, (sens, natural, d, w), [sens_shape, natural, (128, 128)], "prepare"
    )

    lines = slabs * message
    (spectrum,) = call(
        images_kernel, (gathered, sens, natural, extras), [(lines, 128)], "images"
    )
    spectrum = swap(spectrum, slab_axes)
    (mask,) = call(mask_kernel, (place, sampling), [(cols // 128, cols, 128)], "mask", 1)
    flat = (2 * rows, zdim, cols)
    smooth, onward, stats = call(
        smooth_kernel, (place, gathered, d, w, r), [flat, flat, (2, 128)], "smooth", 1
    )
    (back,) = call(
        functools.partial(middle_kernel, zdim=zdim),
        (spectrum, mask, stats, forward, inverse),
        [(lines, 128)],
        "middle",
    )
    back = swap(back, slab_axes)
    (sums,) = call(
        combine_kernel,
        (place, back, sens, smooth, onward, wide),
        [(frames, 2 * rows + 1, zdim, cols)],
        "combine",
        1,
    )
    sums = lax.all_to_all(sums, "coil", 0, 0, tiled=True)

    near, far = ("y", "core"), ("z", "coil")
    new_x, new_r, kept, norms, old = call(
        step_kernel,
        (sums, x.reshape(flat), r.reshape(flat), d.reshape(flat)),
        [flat, flat, flat, (lax.axis_size(near), 1, 128), (1, 128)],
        "step",
    )
    norms = lax.all_to_all(norms, near, 0, 0, tiled=True)
    norms = jnp.broadcast_to(
        jnp.sum(norms, axis=0, keepdims=True), (lax.axis_size(far), 1, 128)
    )
    norms = lax.all_to_all(norms, far, 0, 0, tiled=True)
    new_d, norm = call(
        finish_kernel, (norms, old, kept, d.reshape(flat)), [flat, (1, 128)], "finish"
    )

    def restore(values):
        return jnp.swapaxes(values.reshape(2, 1, rows, zdim, cols), 2, 3)

    return restore(new_x), restore(new_r), restore(new_d), norm[0, 0]


def solution(mesh):
    fine = Mesh(mesh.devices.reshape(8, 8, 2, 4), ("z", "y", "core", "coil"))
    image = P(None, "coil", None, slab_axes, None)
    return jax.shard_map(
        body,
        mesh=fine,
        in_specs=(image, image, image, image, P(), P("coil", None, slab_axes, None)),
        out_specs=(image, image, image, P()),
        check_vma=False,
    )
```

```python
import math

import jax
import jax.numpy as jnp
import ml_dtypes
import numpy as np
from jax import lax
from jax.experimental import pallas as pl
from jax.experimental.pallas import tpu as pltpu
from jax.sharding import Mesh
from jax.sharding import PartitionSpec as P

smooth_scale = 0.05
slab_axes = ("z", "y", "core")
f32 = jnp.float32
bf16 = jnp.bfloat16

message = 18


def dft_tables(length):
    counter = np.arange(length, dtype=np.int64)
    phases = (counter[:, None] * counter[None, :]) % length
    angles = phases.astype(np.float32) * np.float32(2.0 * math.pi / length)
    unit_norm = np.float32(1.0 / math.sqrt(length))
    wide = angles.astype(np.float64)
    cos = np.cos(wide).astype(np.float32) * unit_norm
    sin = np.sin(wide).astype(np.float32) * unit_norm
    return cos.astype(ml_dtypes.bfloat16), sin.astype(ml_dtypes.bfloat16)


def split(values):
    upper = values.astype(bf16)
    return upper, (values - upper.astype(f32)).astype(bf16)


def mm(a, b, contract):
    return lax.dot_general(a, b, (contract, ((), ())), preferred_element_type=f32)


def staggered(count, first, second):
    held, results = first(0), []
    for i in range(count):
        ahead = first(i + 1) if i + 1 < count else None
        results.append(second(i, held))
        held = ahead
    return results


def sens_rows(sens_ref, part, row, coils):
    pieces = [sens_ref[part, c, row].astype(f32) for c in range(coils)]
    return jnp.concatenate(pieces, axis=0)


def relay_kernel(sens_ref, sens_out_ref):
    coils, rows = sens_ref.shape[1:3]
    for p in range(2):
        for r in range(rows):
            sens_out_ref[p, r] = sens_rows(sens_ref, p, r, coils)


def table_kernel(table_ref, out_ref):
    out_ref[...] = table_ref[...]


def images_kernel(all_ref, sens_ref, table_ref, out_ref):
    frames, _, rows, zdim, _ = all_ref.shape
    coils = sens_ref.shape[2] // zdim
    table = table_ref[...]
    table = jnp.concatenate([table, table], axis=1)
    half = table.shape[0] // 2
    groups = half // 128

    def forward(r):
        s_re, s_im = sens_ref[0, r], sens_ref[1, r]
        real, imag = [], []
        for f in range(frames):
            d_re = jnp.concatenate([all_ref[f, 0, r]] * coils, axis=0)
            d_im = jnp.concatenate([all_ref[f, 1, r]] * coils, axis=0)
            real.append(s_re * d_re - s_im * d_im)
            imag.append(s_re * d_im + s_im * d_re)
        upper, lower = split(jnp.concatenate(real + imag, axis=0))
        return mm(table, jnp.concatenate([upper, lower], axis=1), ((1,), (1,)))

    def store(r, got):
        re = got[:half, :128] + got[half:, 128:]
        im = got[:half, 128:] - got[half:, :128]
        for j in range(groups):
            at = (j * rows + r) * 2
            out_ref[pl.ds(at, 128, stride=message), :] = re[j * 128 : (j + 1) * 128]
            out_ref[pl.ds(at + 1, 128, stride=message), :] = im[j * 128 : (j + 1) * 128]

    staggered(rows, forward, store)


def mask_kernel(place_ref, sampling_ref, out_ref):
    frames, full, cols = sampling_ref.shape
    groups = cols // 128
    lane = lax.broadcasted_iota(jnp.int32, (cols, cols), 1)
    freq = lax.broadcasted_iota(jnp.int32, (cols, cols), 0)
    wanted = (lane // 128) * 128 + place_ref[0]
    total = jnp.zeros((full, cols), f32)
    for f in range(frames):
        mine = (freq == wanted) & ((lane % 128) // (128 // frames) == f)
        chosen = jnp.where(mine, 1.0, 0.0).astype(bf16)
        total += mm(sampling_ref[f].astype(f32).astype(bf16), chosen, ((1,), (0,)))
    for j in range(groups):
        out_ref[j] = total[:, j * 128 : (j + 1) * 128]


def edges_kernel(own_ref, weight_ref, last_ref, first_ref):
    rows = weight_ref.shape[0]
    for p in range(2):
        last_ref[p] = own_ref[p, rows - 1]
        first_ref[p] = own_ref[p, 0]
    last_ref[2] = weight_ref[rows - 1].astype(f32)


def smooth_kernel(
    place_ref, all_ref, own_ref, weight_ref, before_ref, after_ref, out_ref, next_ref
):
    slab, frame, slabs, frames = (place_ref[i] for i in range(4))
    rows, zdim, cols = own_ref.shape[1:]
    later = jnp.minimum(frame + 1, frames - 1)
    has_next_row = jnp.where(slab < slabs - 1, 1.0, 0.0)
    has_previous_row = jnp.where(slab > 0, 1.0, 0.0)
    zero_col = jnp.zeros((zdim, 1), f32)
    zero_slice = jnp.zeros((1, cols), f32)
    weights = [weight_ref[r].astype(f32) for r in range(rows)]
    for p in range(2):
        values = [own_ref[p, r] for r in range(rows)]
        flux = (before_ref[2] * has_previous_row) * (values[0] - before_ref[p])
        for r in range(rows):
            v, weight = values[r], weights[r]
            term = flux
            if r < rows - 1:
                flux = weight * (values[r + 1] - v)
            else:
                flux = (weight * has_next_row) * (after_ref[p] - v)
            term -= flux
            onward = smooth_scale * (weight * (all_ref[later, p, r] - v))
            across = weight[:-1] * (v[1:] - v[:-1])
            term += jnp.concatenate([zero_slice, across], axis=0)
            term -= jnp.concatenate([across, zero_slice], axis=0)
            across = weight[:, :-1] * (v[:, 1:] - v[:, :-1])
            term += jnp.concatenate([zero_col, across], axis=1)
            term -= jnp.concatenate([across, zero_col], axis=1)
            out_ref[p * rows + r] = smooth_scale * term - onward
            next_ref[p * rows + r] = onward


def middle_kernel(in_ref, mask_ref, forward_ref, inverse_ref, out_ref):
    groups = mask_ref.shape[0]
    rows = 3
    forward = forward_ref[...]
    forward = jnp.concatenate([forward, forward], axis=1)
    inverse = inverse_ref[...]
    inverse = jnp.concatenate([inverse, inverse], axis=1)
    half = forward.shape[0] // 2

    def gather(j):
        parts = []
        for r in range(rows):
            at = (j * rows + r) * 2
            re = in_ref[pl.ds(at, 128, stride=message), :]
            im = in_ref[pl.ds(at + 1, 128, stride=message), :]
            parts.append(jnp.concatenate([re, im], axis=1))
        upper, lower = split(jnp.concatenate(parts, axis=0))
        return mm(forward, jnp.concatenate([upper, lower], axis=0), ((1,), (0,)))

    def sample(j, got):
        mask = mask_ref[j]
        re = (got[:half, :128] + got[half:, 128:]) * mask
        im = (got[:half, 128:] - got[half:, :128]) * mask
        upper, lower = split(jnp.concatenate([re, im], axis=1))
        back = mm(inverse, jnp.concatenate([upper, lower], axis=0), ((1,), (0,)))
        store(j, back)

    def store(j, got):
        re = got[:half, :128] - got[half:, 128:]
        im = got[:half, 128:] + got[half:, :128]
        for r in range(rows):
            at = (r * groups + j) * 2
            out_ref[pl.ds(at, 128, stride=message), :] = re[r * 128 : (r + 1) * 128]
            out_ref[pl.ds(at + 1, 128, stride=message), :] = im[r * 128 : (r + 1) * 128]

    staggered(groups, gather, sample)


def combine_kernel(place_ref, in_ref, sens_ref, smooth_ref, next_ref, table_ref, out_ref):
    frame, frame_count = place_ref[1], place_ref[3]
    frames, _, zdim, cols = out_ref.shape
    rows, span = sens_ref.shape[1:3]
    table = table_ref[...]
    table = jnp.concatenate([table, table], axis=0)
    groups = cols // 128

    def backward(r):
        real, imag = [], []
        for j in range(groups):
            at = (r * groups + j) * 2
            real.append(in_ref[pl.ds(at, 128, stride=message), :].T)
            imag.append(in_ref[pl.ds(at + 1, 128, stride=message), :].T)
        both = jnp.concatenate(
            [jnp.concatenate(real, axis=1), jnp.concatenate(imag, axis=1)], axis=0
        )
        upper, lower = split(both)
        return mm(jnp.concatenate([upper, lower], axis=1), table, ((1,), (0,)))

    def add_coils(r, got):
        re = got[:128, :cols] - got[128:, cols:]
        im = got[128:, :cols] + got[:128, cols:]
        s_re, s_im = sens_ref[0, r], sens_ref[1, r]
        for f in range(frames):
            b_re = re[f * span : (f + 1) * span]
            b_im = im[f * span : (f + 1) * span]
            for p, t in enumerate((s_re * b_re + s_im * b_im, s_re * b_im - s_im * b_re)):
                eight = t[0:8]
                for g in range(1, span // 8):
                    eight = eight + t[g * 8 : (g + 1) * 8]
                out_ref[f, p * rows + r] = eight[0:zdim] + eight[zdim : 2 * zdim]

    staggered(rows, backward, add_coils)
    for i in range(2 * rows):
        out_ref[frame, i] += smooth_ref[i]

    @pl.when(frame < frame_count - 1)
    def _():
        for i in range(2 * rows):
            out_ref[frame + 1, i] += next_ref[i]


def whole(values):
    return jnp.sum(jnp.sum(values, axis=0, keepdims=True), axis=1, keepdims=True)


def in_lanes(values):
    lane = lax.broadcasted_iota(jnp.int32, (1, 128), 1)
    row = jnp.zeros((1, 128), f32)
    for i, value in enumerate(values):
        row = jnp.where(lane == i, value, row)
    return row


def share(value, weight):
    return jnp.where(weight > 0, value / jnp.where(weight > 0, weight, 1.0), 0.0)


def sums_kernel(sums_ref, residual_ref, direction_ref, applied_ref, out_ref):
    planes = residual_ref.shape[0]
    sources = sums_ref.shape[0]
    zero = jnp.zeros(residual_ref.shape[1:], f32)
    norm, curvature, size, cross, rest = zero, zero, zero, zero, zero
    for i in range(planes):
        value = sums_ref[0, i]
        for k in range(1, sources):
            value = value + sums_ref[k, i]
        applied_ref[i] = value
        r = residual_ref[i]
        norm += r * r
        curvature += direction_ref[i] * value
        size += value * value
        cross += r * value
    size = whole(size)
    ratio = share(whole(cross), size)
    for i in range(planes):
        left = residual_ref[i] - ratio * applied_ref[i]
        rest += left * left
    row = in_lanes([whole(norm), whole(curvature), size, ratio, whole(rest)])
    out_ref[...] = jnp.broadcast_to(row[None], out_ref.shape)


def joined(parts):
    size, ratio = parts[:, 2:3], parts[:, 3:4]
    norm, curvature = whole(parts[:, 0:1]), whole(parts[:, 1:2])
    all_size = whole(size)
    all_ratio = share(whole(size * ratio), all_size)
    away = ratio - all_ratio
    rest = whole(parts[:, 4:5] + (size * away) * away)
    return norm, curvature, all_size, all_ratio, rest


def join_kernel(parts_ref, out_ref):
    row = in_lanes(joined(parts_ref[:, 0, :]))
    out_ref[...] = jnp.broadcast_to(row[None], out_ref.shape)


def finish_kernel(
    parts_ref, applied_ref, iterate_ref, residual_ref, direction_ref, new_iterate_ref, new_residual_ref, new_direction_ref, norm_ref
):
    old_norm, curvature, size, ratio, rest = joined(parts_ref[:, 0, :])
    step = old_norm / curvature
    away = ratio - step
    new_norm = rest + (size * away) * away
    turn = new_norm / old_norm
    for i in range(direction_ref.shape[0]):
        d = direction_ref[i]
        fresh = residual_ref[i] - step * applied_ref[i]
        new_iterate_ref[i] = iterate_ref[i] + step * d
        new_residual_ref[i] = fresh
        new_direction_ref[i] = fresh + turn * d
    norm_ref[...] = jnp.broadcast_to(new_norm, norm_ref.shape)


vmem = pl.BlockSpec(memory_space=pltpu.VMEM)
smem = pl.BlockSpec(memory_space=pltpu.SMEM)


params = pltpu.CompilerParams(vmem_limit_bytes=40 * 1024 * 1024)


def call(kernel, ins, outs, name, scalars=0):
    return pl.pallas_call(
        kernel,
        out_shape=[
            jax.ShapeDtypeStruct(s, f32) if isinstance(s, tuple) else jax.ShapeDtypeStruct(s.shape, s.dtype)
            for s in outs
        ],
        in_specs=[smem] * scalars + [vmem] * (len(ins) - scalars),
        out_specs=[vmem] * len(outs),
        compiler_params=params,
        name=name,
    )(*ins)


def swap(values, axis):
    pairs = values.reshape(values.shape[0] // 2, 2, 128)
    return lax.all_to_all(pairs, axis, 0, 0, tiled=True).reshape(values.shape)


def body(iterate, residual, direction, sensitivity, sampling, edge_weight):
    slabs = lax.axis_size(slab_axes)
    frames = lax.axis_size("coil")
    rows, zdim, cols = direction.shape[3], direction.shape[2], direction.shape[4]

    sens = jnp.swapaxes(sensitivity, 2, 3)
    d = jnp.swapaxes(direction, 2, 3)[:, 0]
    r = jnp.swapaxes(residual, 2, 3)[:, 0]
    x = jnp.swapaxes(iterate, 2, 3)[:, 0]
    w = jnp.swapaxes(edge_weight, 1, 2)[0]

    cos, sin = dft_tables(cols)
    by_slab = np.arange(cols).reshape(cols // rows, rows).T.reshape(-1)
    natural = jnp.asarray(np.concatenate([cos, sin], axis=0))
    forward = jnp.asarray(np.concatenate([cos[:, by_slab], sin[:, by_slab]], axis=0))
    inverse = jnp.asarray(np.concatenate([cos[by_slab], sin[by_slab]], axis=0))
    wide = jnp.asarray(np.concatenate([cos, sin], axis=1))

    place = jnp.stack(
        [lax.axis_index(slab_axes), lax.axis_index("coil"), jnp.int32(slabs), jnp.int32(frames)]
    ).astype(jnp.int32)
    copies = jnp.broadcast_to(d[None], (frames,) + d.shape)
    gathered = lax.all_to_all(copies, "coil", 0, 0, tiled=True)
    sens_shape = (2, rows, sens.shape[1] * zdim, cols)
    (sens,) = call(relay_kernel, (sens,), [sens_shape], "relay")
    (natural,) = call(table_kernel, (natural,), [natural], "table")

    lines = slabs * message
    (spectrum,) = call(images_kernel, (gathered, sens, natural), [(lines, 128)], "images")
    spectrum = swap(spectrum, slab_axes)
    last, first = call(edges_kernel, (d, w), [(3, zdim, cols), (2, zdim, cols)], "edges")
    up = [(i, i + 1) for i in range(slabs - 1)]
    before = lax.ppermute(last, slab_axes, up)
    after = lax.ppermute(first, slab_axes, [(j, i) for i, j in up])
    (mask,) = call(mask_kernel, (place, sampling), [(cols // 128, cols, 128)], "mask", 1)
    flat = (2 * rows, zdim, cols)
    smooth, onward = call(
        smooth_kernel, (place, gathered, d, w, before, after), [flat, flat], "smooth", 1
    )
    spectrum, smooth, onward = lax.optimization_barrier((spectrum, smooth, onward))
    (back,) = call(
        middle_kernel, (spectrum, mask, forward, inverse), [(lines, 128)], "middle"
    )
    back = swap(back, slab_axes)
    (sums,) = call(
        combine_kernel,
        (place, back, sens, smooth, onward, wide),
        [(frames,) + flat],
        "combine",
        1,
    )
    sums = lax.all_to_all(sums, "coil", 0, 0, tiled=True)

    near, far = ("y", "core"), ("z", "coil")
    x, r, d = (v.reshape(flat) for v in (x, r, d))
    applied, parts = call(
        sums_kernel, (sums, r, d), [flat, (lax.axis_size(near), 1, 128)], "sums"
    )
    parts = lax.all_to_all(parts, near, 0, 0, tiled=True)
    (parts,) = call(join_kernel, (parts,), [(lax.axis_size(far), 1, 128)], "join")
    parts = lax.all_to_all(parts, far, 0, 0, tiled=True)
    new_x, new_r, new_d, norm = call(
        finish_kernel, (parts, applied, x, r, d), [flat, flat, flat, (1, 128)], "finish"
    )

    def restore(values):
        return jnp.swapaxes(values.reshape(2, 1, rows, zdim, cols), 2, 3)

    return restore(new_x), restore(new_r), restore(new_d), norm[0, 0]


def solution(mesh):
    fine = Mesh(mesh.devices.reshape(8, 8, 2, 4), ("z", "y", "core", "coil"))
    image = P(None, "coil", None, slab_axes, None)
    return jax.shard_map(
        body,
        mesh=fine,
        in_specs=(image, image, image, image, P(), P("coil", None, slab_axes, None)),
        out_specs=(image, image, image, P()),
        check_vma=False,
    )
```

```python
import math

import jax
import jax.numpy as jnp
import ml_dtypes
import numpy as np
from jax import lax
from jax.experimental import pallas as pl
from jax.experimental.pallas import tpu as pltpu
from jax.sharding import Mesh
from jax.sharding import PartitionSpec as P

smooth_scale = 0.05
slab_axes = ("z", "y", "core")
f32 = jnp.float32
bf16 = jnp.bfloat16

message = 18

rows, coils = 3, 8
at_direction = 2 * rows * coils
at_residual = at_direction + 2 * rows
at_smooth = at_residual + 2 * rows
at_weight = at_smooth + 2 * rows
told = 72


def dft_tables(length):
    counter = np.arange(length, dtype=np.int64)
    phases = (counter[:, None] * counter[None, :]) % length
    angles = phases.astype(np.float32) * np.float32(2.0 * math.pi / length)
    unit_norm = np.float32(1.0 / math.sqrt(length))
    wide = angles.astype(np.float64)
    cos = np.cos(wide).astype(np.float32) * unit_norm
    sin = np.sin(wide).astype(np.float32) * unit_norm
    return cos.astype(ml_dtypes.bfloat16), sin.astype(ml_dtypes.bfloat16)


def split(values):
    upper = values.astype(bf16)
    return upper, (values - upper.astype(f32)).astype(bf16)


def mm(a, b, contract):
    return lax.dot_general(a, b, (contract, ((), ())), preferred_element_type=f32)


def staggered(count, first, second):
    held, results = first(0), []
    for i in range(count):
        ahead = first(i + 1) if i + 1 < count else None
        results.append(second(i, held))
        held = ahead
    return results


def sens_rows(all_ref, part, row):
    at = (part * rows + row) * coils
    return jnp.concatenate([all_ref[k, at : at + coils] for k in range(all_ref.shape[0])], axis=0)


def tell_kernel(*refs):
    sources, out_ref, held, done = refs[:4], refs[4], refs[5:9], refs[9]
    copies = [pltpu.make_async_copy(sources[i], held[i], done.at[i]) for i in range(4)]
    for copy in copies:
        copy.start()
    for copy in copies:
        copy.wait()
    sens_ref, direction_ref, residual_ref, weight_ref = held
    slices, _, cols = out_ref.shape
    zero_slice = jnp.zeros((1, cols), f32)

    def put(row, values):
        for z in range(slices):
            out_ref[z, row : row + 1] = values[z : z + 1]

    for r in range(rows):
        weight = weight_ref[r].astype(f32)
        put(at_weight + r, weight)
        for p in range(2):
            i = p * rows + r
            tiles = [sens_ref[p, c, r].astype(f32) for c in range(coils)]
            for z in range(slices):
                out_ref[z, i * coils : (i + 1) * coils] = jnp.concatenate(
                    [t[z : z + 1] for t in tiles], axis=0
                )
            v = direction_ref[p, r]
            put(at_direction + i, v)
            put(at_residual + i, residual_ref[p, r])
            flux = weight[:-1] * (v[1:] - v[:-1])
            put(
                at_smooth + i,
                jnp.concatenate([zero_slice, flux], axis=0)
                - jnp.concatenate([flux, zero_slice], axis=0),
            )
    for z in range(slices):
        out_ref[z, at_weight + rows :] = jnp.zeros((told - at_weight - rows, cols), f32)


def table_kernel(table_ref, out_ref):
    out_ref[...] = table_ref[...]


def images_kernel(all_ref, table_ref, out_ref):
    frames, _, cols = all_ref.shape
    table = table_ref[...]
    table = jnp.concatenate([table, table], axis=1)
    half = table.shape[0] // 2
    groups = half // 128

    def forward(r):
        s_re, s_im = sens_rows(all_ref, 0, r), sens_rows(all_ref, 1, r)
        real, imag = [], []
        for f in range(frames):
            at = at_direction + r
            d_re = jnp.broadcast_to(all_ref[f, at : at + 1], s_re.shape)
            d_im = jnp.broadcast_to(all_ref[f, at + rows : at + rows + 1], s_re.shape)
            real.append(s_re * d_re - s_im * d_im)
            imag.append(s_re * d_im + s_im * d_re)
        upper, lower = split(jnp.concatenate(real + imag, axis=0))
        return mm(table, jnp.concatenate([upper, lower], axis=1), ((1,), (1,)))

    def store(r, got):
        re = got[:half, :128] + got[half:, 128:]
        im = got[:half, 128:] - got[half:, :128]
        for j in range(groups):
            at = (j * rows + r) * 2
            out_ref[pl.ds(at, 128, stride=message), :] = re[j * 128 : (j + 1) * 128]
            out_ref[pl.ds(at + 1, 128, stride=message), :] = im[j * 128 : (j + 1) * 128]

    staggered(rows, forward, store)


def mask_kernel(place_ref, sampling_ref, out_ref):
    frames, full, cols = sampling_ref.shape
    groups = cols // 128
    lane = lax.broadcasted_iota(jnp.int32, (cols, cols), 1)
    freq = lax.broadcasted_iota(jnp.int32, (cols, cols), 0)
    wanted = (lane // 128) * 128 + place_ref[0]
    total = jnp.zeros((full, cols), f32)
    for f in range(frames):
        mine = (freq == wanted) & ((lane % 128) // (128 // frames) == f)
        chosen = jnp.where(mine, 1.0, 0.0).astype(bf16)
        total += mm(sampling_ref[f].astype(f32).astype(bf16), chosen, ((1,), (0,)))
    for j in range(groups):
        out_ref[j] = total[:, j * 128 : (j + 1) * 128]


def edges_kernel(all_ref, last_ref, first_ref):
    for f in range(all_ref.shape[0]):
        for p in range(2):
            at = at_direction + p * rows
            last_ref[f, p : p + 1] = all_ref[f, at + rows - 1 : at + rows]
            first_ref[f, p : p + 1] = all_ref[f, at : at + 1]
        last_ref[f, 2:3] = all_ref[f, at_weight + rows - 1 : at_weight + rows]


def smooth_kernel(place_ref, all_ref, before_ref, after_ref, out_ref):
    slab, slabs = place_ref[0], place_ref[1]
    frames, _, cols = all_ref.shape
    has_next_row = jnp.where(slab < slabs - 1, 1.0, 0.0)
    has_previous_row = jnp.where(slab > 0, 1.0, 0.0)
    zero_col = jnp.zeros((rows, 1), f32)
    for p in range(2):
        at = at_direction + p * rows
        from_frame = None
        for f in range(frames):
            v = all_ref[f, at : at + rows]
            weight = all_ref[f, at_weight : at_weight + rows]
            term = all_ref[f, at_smooth + p * rows : at_smooth + (p + 1) * rows]
            if from_frame is not None:
                term = term + from_frame
            if f < frames - 1:
                from_frame = weight * (all_ref[f + 1, at : at + rows] - v)
                term = term - from_frame
            flux = weight[:, :-1] * (v[:, 1:] - v[:, :-1])
            term += jnp.concatenate([zero_col, flux], axis=1)
            term -= jnp.concatenate([flux, zero_col], axis=1)
            previous = before_ref[f, p : p + 1]
            following = after_ref[f, p : p + 1]
            first = (before_ref[f, 2:3] * has_previous_row) * (v[0:1] - previous)
            inner = weight[:-1] * (v[1:] - v[:-1])
            final = (weight[-1:] * has_next_row) * (following - v[-1:])
            term += jnp.concatenate([first, inner], axis=0)
            term -= jnp.concatenate([inner, final], axis=0)
            out_ref[f, p * rows : (p + 1) * rows] = smooth_scale * term


def middle_kernel(in_ref, mask_ref, forward_ref, inverse_ref, out_ref):
    groups = mask_ref.shape[0]
    forward = forward_ref[...]
    forward = jnp.concatenate([forward, forward], axis=1)
    inverse = inverse_ref[...]
    inverse = jnp.concatenate([inverse, inverse], axis=1)
    half = forward.shape[0] // 2

    def gather(j):
        parts = []
        for r in range(rows):
            at = (j * rows + r) * 2
            re = in_ref[pl.ds(at, 128, stride=message), :]
            im = in_ref[pl.ds(at + 1, 128, stride=message), :]
            parts.append(jnp.concatenate([re, im], axis=1))
        upper, lower = split(jnp.concatenate(parts, axis=0))
        return mm(forward, jnp.concatenate([upper, lower], axis=0), ((1,), (0,)))

    def sample(j, got):
        mask = mask_ref[j]
        re = (got[:half, :128] + got[half:, 128:]) * mask
        im = (got[:half, 128:] - got[half:, :128]) * mask
        upper, lower = split(jnp.concatenate([re, im], axis=1))
        back = mm(inverse, jnp.concatenate([upper, lower], axis=0), ((1,), (0,)))
        store(j, back)

    def store(j, got):
        re = got[:half, :128] - got[half:, 128:]
        im = got[:half, 128:] + got[half:, :128]
        for r in range(rows):
            at = (r * groups + j) * 2
            out_ref[pl.ds(at, 128, stride=message), :] = re[r * 128 : (r + 1) * 128]
            out_ref[pl.ds(at + 1, 128, stride=message), :] = im[r * 128 : (r + 1) * 128]

    staggered(groups, gather, sample)


def whole(values):
    return jnp.sum(jnp.sum(values, axis=0, keepdims=True), axis=1, keepdims=True)


def in_lanes(values):
    lane = lax.broadcasted_iota(jnp.int32, (1, 128), 1)
    row = jnp.zeros((1, 128), f32)
    for i, value in enumerate(values):
        row = jnp.where(lane == i, value, row)
    return row


def share(value, weight):
    return jnp.where(weight > 0, value / jnp.where(weight > 0, weight, 1.0), 0.0)


def combine_kernel(in_ref, all_ref, smooth_ref, table_ref, applied_ref, out_ref):
    frames, _, cols = all_ref.shape
    table = table_ref[...]
    table = jnp.concatenate([table, table], axis=0)
    groups = cols // 128
    span = 128 // frames
    zero = jnp.zeros((1, cols), f32)

    def backward(r):
        real, imag = [], []
        for j in range(groups):
            at = (r * groups + j) * 2
            real.append(in_ref[pl.ds(at, 128, stride=message), :].T)
            imag.append(in_ref[pl.ds(at + 1, 128, stride=message), :].T)
        both = jnp.concatenate(
            [jnp.concatenate(real, axis=1), jnp.concatenate(imag, axis=1)], axis=0
        )
        upper, lower = split(both)
        return mm(jnp.concatenate([upper, lower], axis=1), table, ((1,), (0,)))

    def add_coils(r, got):
        re = got[:128, :cols] - got[128:, cols:]
        im = got[128:, :cols] + got[:128, cols:]
        s_re, s_im = sens_rows(all_ref, 0, r), sens_rows(all_ref, 1, r)
        for f in range(frames):
            b_re = re[f * span : (f + 1) * span]
            b_im = im[f * span : (f + 1) * span]
            for p, t in enumerate((s_re * b_re + s_im * b_im, s_re * b_im - s_im * b_re)):
                i = p * rows + r
                total = jnp.sum(t, axis=0, keepdims=True)
                applied_ref[f, i : i + 1] = total + smooth_ref[f, i : i + 1]

    staggered(rows, backward, add_coils)
    six = 2 * rows
    zero = jnp.zeros((six, cols), f32)
    norm, curvature, size, cross, rest = zero, zero, zero, zero, zero
    for f in range(frames):
        value = applied_ref[f, 0:six]
        r = all_ref[f, at_residual : at_residual + six]
        norm += r * r
        curvature += all_ref[f, at_direction : at_direction + six] * value
        size += value * value
        cross += r * value
    size = whole(size)
    ratio = share(whole(cross), size)
    for f in range(frames):
        left = all_ref[f, at_residual : at_residual + six] - ratio * applied_ref[f, 0:six]
        rest += left * left
        applied_ref[f, six:] = jnp.zeros((applied_ref.shape[1] - six, cols), f32)
    row = in_lanes([whole(norm), whole(curvature), size, ratio, whole(rest)])
    out_ref[...] = jnp.broadcast_to(row[None], out_ref.shape)


def joined(parts):
    size, ratio = parts[:, 2:3], parts[:, 3:4]
    norm, curvature = whole(parts[:, 0:1]), whole(parts[:, 1:2])
    all_size = whole(size)
    all_ratio = share(whole(size * ratio), all_size)
    away = ratio - all_ratio
    rest = whole(parts[:, 4:5] + (size * away) * away)
    return norm, curvature, all_size, all_ratio, rest


def join_kernel(parts_ref, applied_ref, out_ref):
    row = in_lanes(joined(parts_ref[:, 0, :]))
    out_ref[...] = applied_ref[...]
    for f in range(out_ref.shape[0]):
        out_ref[f, 2 * rows : 2 * rows + 1, 0:128] = row


def finish_kernel(
    all_ref, iterate_ref, residual_ref, direction_ref, new_iterate_ref, new_residual_ref, new_direction_ref, norm_ref
):
    slices = all_ref.shape[0]
    parts = [all_ref[z, 2 * rows : 2 * rows + 1, 0:128] for z in range(slices)]
    old_norm, curvature, size, ratio, rest = joined(jnp.concatenate(parts, axis=0))
    step = old_norm / curvature
    away = ratio - step
    new_norm = rest + (size * away) * away
    turn = new_norm / old_norm
    for i in range(direction_ref.shape[0]):
        d = direction_ref[i]
        applied = jnp.concatenate([all_ref[z, i : i + 1] for z in range(slices)], axis=0)
        fresh = residual_ref[i] - step * applied
        new_iterate_ref[i] = iterate_ref[i] + step * d
        new_residual_ref[i] = fresh
        new_direction_ref[i] = fresh + turn * d
    norm_ref[...] = jnp.broadcast_to(new_norm, norm_ref.shape)


vmem = pl.BlockSpec(memory_space=pltpu.VMEM)
smem = pl.BlockSpec(memory_space=pltpu.SMEM)
hbm = pl.BlockSpec(memory_space=pltpu.HBM)


params = pltpu.CompilerParams(vmem_limit_bytes=40 * 1024 * 1024)


def call(kernel, ins, outs, name, scalars=0):
    return pl.pallas_call(
        kernel,
        out_shape=[
            jax.ShapeDtypeStruct(s, f32) if isinstance(s, tuple) else jax.ShapeDtypeStruct(s.shape, s.dtype)
            for s in outs
        ],
        in_specs=[smem] * scalars + [vmem] * (len(ins) - scalars),
        out_specs=[vmem] * len(outs),
        compiler_params=params,
        name=name,
    )(*ins)


def tell(arrays, slices, cols):
    return pl.pallas_call(
        tell_kernel,
        out_shape=jax.ShapeDtypeStruct((slices, told, cols), f32),
        in_specs=[hbm] * len(arrays),
        out_specs=vmem,
        scratch_shapes=[pltpu.VMEM(a.shape, a.dtype) for a in arrays]
        + [pltpu.SemaphoreType.DMA((len(arrays),))],
        compiler_params=pltpu.CompilerParams(vmem_limit_bytes=65_000_000),
        name="tell",
    )(*arrays)


def swap(values, axis):
    pairs = values.reshape(values.shape[0] // 2, 2, 128)
    return lax.all_to_all(pairs, axis, 0, 0, tiled=True).reshape(values.shape)


def body(iterate, residual, direction, sensitivity, sampling, edge_weight):
    slabs = lax.axis_size(slab_axes)
    frames = lax.axis_size("coil")
    zdim, cols = direction.shape[2], direction.shape[4]

    sens = jnp.swapaxes(sensitivity, 2, 3)
    d = jnp.swapaxes(direction, 2, 3)[:, 0]
    r = jnp.swapaxes(residual, 2, 3)[:, 0]
    x = jnp.swapaxes(iterate, 2, 3)[:, 0]
    w = jnp.swapaxes(edge_weight, 1, 2)[0]

    cos, sin = dft_tables(cols)
    by_slab = np.arange(cols).reshape(cols // rows, rows).T.reshape(-1)
    natural = jnp.asarray(np.concatenate([cos, sin], axis=0))
    forward = jnp.asarray(np.concatenate([cos[:, by_slab], sin[:, by_slab]], axis=0))
    inverse = jnp.asarray(np.concatenate([cos[by_slab], sin[by_slab]], axis=0))
    wide = jnp.asarray(np.concatenate([cos, sin], axis=1))

    place = jnp.stack([lax.axis_index(slab_axes), jnp.int32(slabs)]).astype(jnp.int32)
    mine = lax.all_to_all(tell((sens, d, r, w), zdim, cols), "coil", 0, 0, tiled=True)
    (natural,) = call(table_kernel, (natural,), [natural], "table")

    lines = slabs * message
    (spectrum,) = call(images_kernel, (mine, natural), [(lines, 128)], "images")
    spectrum = swap(spectrum, slab_axes)
    last, first = call(edges_kernel, (mine,), [(frames, 3, cols), (frames, 2, cols)], "edges")
    up = [(i, i + 1) for i in range(slabs - 1)]
    before = lax.ppermute(last, slab_axes, up)
    after = lax.ppermute(first, slab_axes, [(j, i) for i, j in up])
    (mask,) = call(mask_kernel, (place, sampling), [(cols // 128, cols, 128)], "mask", 1)
    (smooth,) = call(
        smooth_kernel, (place, mine, before, after), [(frames, 2 * rows, cols)], "smooth", 1
    )
    spectrum, smooth = lax.optimization_barrier((spectrum, smooth))
    (back,) = call(
        middle_kernel, (spectrum, mask, forward, inverse), [(lines, 128)], "middle"
    )
    back = swap(back, slab_axes)
    applied, parts = call(
        combine_kernel,
        (back, mine, smooth, wide),
        [(frames, 8, cols), (slabs, 1, 128)],
        "combine",
    )
    parts = lax.all_to_all(parts, slab_axes, 0, 0, tiled=True)
    (applied,) = call(join_kernel, (parts, applied), [applied], "join")
    applied = lax.all_to_all(applied, "coil", 0, 0, tiled=True)

    flat = (2 * rows, zdim, cols)
    x, r, d = (v.reshape(flat) for v in (x, r, d))
    new_x, new_r, new_d, norm = call(
        finish_kernel, (applied, x, r, d), [flat, flat, flat, (1, 128)], "finish"
    )

    def restore(values):
        return jnp.swapaxes(values.reshape(2, 1, rows, zdim, cols), 2, 3)

    return restore(new_x), restore(new_r), restore(new_d), norm[0, 0]


def solution(mesh):
    fine = Mesh(mesh.devices.reshape(8, 8, 2, 4), ("z", "y", "core", "coil"))
    image = P(None, "coil", None, slab_axes, None)
    return jax.shard_map(
        body,
        mesh=fine,
        in_specs=(image, image, image, image, P(), P("coil", None, slab_axes, None)),
        out_specs=(image, image, image, P()),
        check_vma=False,
    )
```

```python
import math

import jax
import jax.numpy as jnp
import ml_dtypes
import numpy as np
from jax import lax
from jax.experimental import pallas as pl
from jax.experimental.pallas import tpu as pltpu
from jax.sharding import Mesh
from jax.sharding import PartitionSpec as P

smooth_scale = 0.05
slab_axes = ("z", "y", "core")
swap_axes = ("z", "core", "y")
f32 = jnp.float32
bf16 = jnp.bfloat16

message = 18

rows, coils = 3, 8
at_direction = 2 * rows * coils
at_edge = at_direction + 2 * rows
told = at_edge + 2
at_smooth = 2 * rows
at_weight = 4 * rows
told_later = 16


def dft_tables(length):
    counter = np.arange(length, dtype=np.int64)
    phases = (counter[:, None] * counter[None, :]) % length
    angles = phases.astype(np.float32) * np.float32(2.0 * math.pi / length)
    unit_norm = np.float32(1.0 / math.sqrt(length))
    wide = angles.astype(np.float64)
    cos = np.cos(wide).astype(np.float32) * unit_norm
    sin = np.sin(wide).astype(np.float32) * unit_norm
    return cos.astype(ml_dtypes.bfloat16), sin.astype(ml_dtypes.bfloat16)


def split(values):
    upper = values.astype(bf16)
    return upper, (values - upper.astype(f32)).astype(bf16)


def mm(a, b, contract):
    return lax.dot_general(a, b, (contract, ((), ())), preferred_element_type=f32)


def staggered(count, first, second):
    held, results = first(0), []
    for i in range(count):
        ahead = first(i + 1) if i + 1 < count else None
        results.append(second(i, held))
        held = ahead
    return results


def sens_rows(all_ref, part, row):
    at = (part * rows + row) * coils
    return jnp.concatenate([all_ref[k, at : at + coils] for k in range(all_ref.shape[0])], axis=0)


def tell_kernel(*refs):
    sources, out_ref, held, done = refs[:3], refs[3], refs[4:7], refs[7]
    copies = [pltpu.make_async_copy(sources[i], held[i], done.at[i]) for i in range(3)]
    for copy in copies:
        copy.start()
    for copy in copies:
        copy.wait()
    sens_ref, direction_ref, weight_ref = held
    slices, _, cols = out_ref.shape

    def put(row, values):
        for z in range(slices):
            out_ref[z, row : row + 1] = values[z : z + 1]

    for p in range(2):
        for r in range(rows):
            i = p * rows + r
            tiles = [sens_ref[p, c, r].astype(f32) for c in range(coils)]
            for z in range(slices):
                out_ref[z, i * coils : (i + 1) * coils] = jnp.concatenate(
                    [t[z : z + 1] for t in tiles], axis=0
                )
            put(at_direction + i, direction_ref[p, r])
    put(at_edge, weight_ref[rows - 1].astype(f32))
    put(at_edge + 1, jnp.zeros((slices, cols), f32))


def later_kernel(place_ref, direction_ref, residual_ref, weight_ref, *refs):
    out_refs, held_ref = refs[:-1], refs[-1]
    plane, planes = place_ref[3], len(out_refs)
    cols = direction_ref.shape[3]
    zero_slice = jnp.zeros((1, cols), f32)
    for r in range(rows):
        weight = weight_ref[r].astype(f32)
        held_ref[at_weight + r] = weight
        for p in range(2):
            i = p * rows + r
            v = direction_ref[p, r]
            held_ref[i] = residual_ref[p, r]
            flux = weight[:-1] * (v[1:] - v[:-1])
            held_ref[at_smooth + i] = jnp.concatenate([zero_slice, flux], axis=0) - jnp.concatenate(
                [flux, zero_slice], axis=0
            )
    for k in range(planes):
        z = lax.rem(plane + k, planes)
        for i in range(at_weight + rows):
            out_refs[k][i : i + 1] = held_ref[i, pl.ds(z, 1), :]
        out_refs[k][at_weight + rows :] = jnp.zeros((told_later - at_weight - rows, cols), f32)


def table_kernel(table_ref, out_ref):
    out_ref[...] = table_ref[...]


def images_kernel(all_ref, table_ref, out_ref):
    frames, _, cols = all_ref.shape
    table = table_ref[...]
    table = jnp.concatenate([table, table], axis=1)
    half = table.shape[0] // 2
    groups = half // 128

    def forward(r):
        s_re, s_im = sens_rows(all_ref, 0, r), sens_rows(all_ref, 1, r)
        real, imag = [], []
        for f in range(frames):
            at = at_direction + r
            d_re = jnp.broadcast_to(all_ref[f, at : at + 1], s_re.shape)
            d_im = jnp.broadcast_to(all_ref[f, at + rows : at + rows + 1], s_re.shape)
            real.append(s_re * d_re - s_im * d_im)
            imag.append(s_re * d_im + s_im * d_re)
        upper, lower = split(jnp.concatenate(real + imag, axis=0))
        return mm(table, jnp.concatenate([upper, lower], axis=1), ((1,), (1,)))

    def store(r, got):
        re = got[:half, :128] + got[half:, 128:]
        im = got[:half, 128:] - got[half:, :128]
        for j in range(groups):
            at = (j * rows + r) * 2
            out_ref[pl.ds(at, 128, stride=message), :] = re[j * 128 : (j + 1) * 128]
            out_ref[pl.ds(at + 1, 128, stride=message), :] = im[j * 128 : (j + 1) * 128]

    staggered(rows, forward, store)


def mask_kernel(place_ref, sampling_ref, out_ref):
    frames, full, cols = sampling_ref.shape
    groups = cols // 128
    lane = lax.broadcasted_iota(jnp.int32, (cols, cols), 1)
    freq = lax.broadcasted_iota(jnp.int32, (cols, cols), 0)
    wanted = (lane // 128) * 128 + place_ref[0]
    total = jnp.zeros((full, cols), f32)
    for f in range(frames):
        mine = (freq == wanted) & ((lane % 128) // (128 // frames) == f)
        chosen = jnp.where(mine, 1.0, 0.0).astype(bf16)
        total += mm(sampling_ref[f].astype(f32).astype(bf16), chosen, ((1,), (0,)))
    for j in range(groups):
        out_ref[j] = total[:, j * 128 : (j + 1) * 128]


def edges_kernel(all_ref, last_ref, first_ref):
    for f in range(all_ref.shape[0]):
        for p in range(2):
            at = at_direction + p * rows
            last_ref[f, p : p + 1] = all_ref[f, at + rows - 1 : at + rows]
            first_ref[f, p : p + 1] = all_ref[f, at : at + 1]
        last_ref[f, 2:3] = all_ref[f, at_edge : at_edge + 1]


def smooth_kernel(place_ref, all_ref, before_ref, after_ref, *refs):
    later_refs, out_ref, residual_ref, later_ref = refs[:-3], *refs[-3:]
    slab, slabs, plane = place_ref[1], place_ref[2], place_ref[3]
    frames, _, cols = all_ref.shape
    for k in range(frames):
        later_ref[lax.rem(plane + frames - k, frames)] = later_refs[k][...]
    residual_ref[...] = later_ref[:, : 2 * rows]
    has_next_row = jnp.where(slab < slabs - 1, 1.0, 0.0)
    has_previous_row = jnp.where(slab > 0, 1.0, 0.0)
    zero_col = jnp.zeros((rows, 1), f32)
    for p in range(2):
        at = at_direction + p * rows
        from_frame = None
        for f in range(frames):
            v = all_ref[f, at : at + rows]
            weight = later_ref[f, at_weight : at_weight + rows]
            term = later_ref[f, at_smooth + p * rows : at_smooth + (p + 1) * rows]
            if from_frame is not None:
                term = term + from_frame
            if f < frames - 1:
                from_frame = weight * (all_ref[f + 1, at : at + rows] - v)
                term = term - from_frame
            flux = weight[:, :-1] * (v[:, 1:] - v[:, :-1])
            term += jnp.concatenate([zero_col, flux], axis=1)
            term -= jnp.concatenate([flux, zero_col], axis=1)
            previous = before_ref[f, p : p + 1]
            following = after_ref[f, p : p + 1]
            first = (before_ref[f, 2:3] * has_previous_row) * (v[0:1] - previous)
            inner = weight[:-1] * (v[1:] - v[:-1])
            final = (weight[-1:] * has_next_row) * (following - v[-1:])
            term += jnp.concatenate([first, inner], axis=0)
            term -= jnp.concatenate([inner, final], axis=0)
            out_ref[f, p * rows : (p + 1) * rows] = smooth_scale * term


def middle_kernel(in_ref, mask_ref, forward_ref, inverse_ref, out_ref):
    groups = mask_ref.shape[0]
    forward = forward_ref[...]
    forward = jnp.concatenate([forward, forward], axis=1)
    inverse = inverse_ref[...]
    inverse = jnp.concatenate([inverse, inverse], axis=1)
    half = forward.shape[0] // 2

    def gather(j):
        parts = []
        for r in range(rows):
            at = (j * rows + r) * 2
            re = in_ref[pl.ds(at, 128, stride=message), :]
            im = in_ref[pl.ds(at + 1, 128, stride=message), :]
            parts.append(jnp.concatenate([re, im], axis=1))
        upper, lower = split(jnp.concatenate(parts, axis=0))
        return mm(forward, jnp.concatenate([upper, lower], axis=0), ((1,), (0,)))

    def sample(j, got):
        mask = mask_ref[j]
        re = (got[:half, :128] + got[half:, 128:]) * mask
        im = (got[:half, 128:] - got[half:, :128]) * mask
        upper, lower = split(jnp.concatenate([re, im], axis=1))
        back = mm(inverse, jnp.concatenate([upper, lower], axis=0), ((1,), (0,)))
        store(j, back)

    def store(j, got):
        re = got[:half, :128] - got[half:, 128:]
        im = got[:half, 128:] + got[half:, :128]
        for r in range(rows):
            at = (r * groups + j) * 2
            out_ref[pl.ds(at, 128, stride=message), :] = re[r * 128 : (r + 1) * 128]
            out_ref[pl.ds(at + 1, 128, stride=message), :] = im[r * 128 : (r + 1) * 128]

    staggered(groups, gather, sample)


def whole(values):
    return jnp.sum(jnp.sum(values, axis=0, keepdims=True), axis=1, keepdims=True)


def in_lanes(values):
    lane = lax.broadcasted_iota(jnp.int32, (1, 128), 1)
    row = jnp.zeros((1, 128), f32)
    for i, value in enumerate(values):
        row = jnp.where(lane == i, value, row)
    return row


def share(value, weight):
    return jnp.where(weight > 0, value / jnp.where(weight > 0, weight, 1.0), 0.0)


def combine_kernel(in_ref, all_ref, smooth_ref, residual_ref, table_ref, applied_ref, out_ref):
    frames, _, cols = all_ref.shape
    table = table_ref[...]
    table = jnp.concatenate([table, table], axis=0)
    groups = cols // 128
    span = 128 // frames
    zero = jnp.zeros((1, cols), f32)

    def backward(r):
        real, imag = [], []
        for j in range(groups):
            at = (r * groups + j) * 2
            real.append(in_ref[pl.ds(at, 128, stride=message), :].T)
            imag.append(in_ref[pl.ds(at + 1, 128, stride=message), :].T)
        both = jnp.concatenate(
            [jnp.concatenate(real, axis=1), jnp.concatenate(imag, axis=1)], axis=0
        )
        upper, lower = split(both)
        return mm(jnp.concatenate([upper, lower], axis=1), table, ((1,), (0,)))

    def add_coils(r, got):
        re = got[:128, :cols] - got[128:, cols:]
        im = got[128:, :cols] + got[:128, cols:]
        s_re, s_im = sens_rows(all_ref, 0, r), sens_rows(all_ref, 1, r)
        for f in range(frames):
            b_re = re[f * span : (f + 1) * span]
            b_im = im[f * span : (f + 1) * span]
            for p, t in enumerate((s_re * b_re + s_im * b_im, s_re * b_im - s_im * b_re)):
                i = p * rows + r
                total = jnp.sum(t, axis=0, keepdims=True)
                applied_ref[f, i : i + 1] = total + smooth_ref[f, i : i + 1]

    staggered(rows, backward, add_coils)
    six = 2 * rows
    zero = jnp.zeros((six, cols), f32)
    norm, curvature, size, cross, rest = zero, zero, zero, zero, zero
    for f in range(frames):
        value = applied_ref[f, 0:six]
        r = residual_ref[f]
        norm += r * r
        curvature += all_ref[f, at_direction : at_direction + six] * value
        size += value * value
        cross += r * value
    size = whole(size)
    ratio = share(whole(cross), size)
    for f in range(frames):
        left = residual_ref[f] - ratio * applied_ref[f, 0:six]
        rest += left * left
        applied_ref[f, six:] = jnp.zeros((applied_ref.shape[1] - six, cols), f32)
    row = in_lanes([whole(norm), whole(curvature), size, ratio, whole(rest)])
    out_ref[...] = jnp.broadcast_to(row[None], out_ref.shape)


def joined(parts):
    size, ratio = parts[:, 2:3], parts[:, 3:4]
    norm, curvature = whole(parts[:, 0:1]), whole(parts[:, 1:2])
    all_size = whole(size)
    all_ratio = share(whole(size * ratio), all_size)
    away = ratio - all_ratio
    rest = whole(parts[:, 4:5] + (size * away) * away)
    return norm, curvature, all_size, all_ratio, rest


def join_kernel(parts_ref, applied_ref, out_ref):
    row = in_lanes(joined(parts_ref[:, 0, :]))
    out_ref[...] = applied_ref[...]
    for f in range(out_ref.shape[0]):
        out_ref[f, 2 * rows : 2 * rows + 1, 0:128] = row


def finish_kernel(
    all_ref, iterate_ref, residual_ref, direction_ref, new_iterate_ref, new_residual_ref, new_direction_ref, norm_ref
):
    slices = all_ref.shape[0]
    parts = [all_ref[z, 2 * rows : 2 * rows + 1, 0:128] for z in range(slices)]
    old_norm, curvature, size, ratio, rest = joined(jnp.concatenate(parts, axis=0))
    step = old_norm / curvature
    away = ratio - step
    new_norm = rest + (size * away) * away
    turn = new_norm / old_norm
    for i in range(direction_ref.shape[0]):
        d = direction_ref[i]
        applied = jnp.concatenate([all_ref[z, i : i + 1] for z in range(slices)], axis=0)
        fresh = residual_ref[i] - step * applied
        new_iterate_ref[i] = iterate_ref[i] + step * d
        new_residual_ref[i] = fresh
        new_direction_ref[i] = fresh + turn * d
    norm_ref[...] = jnp.broadcast_to(new_norm, norm_ref.shape)


vmem = pl.BlockSpec(memory_space=pltpu.VMEM)
smem = pl.BlockSpec(memory_space=pltpu.SMEM)
hbm = pl.BlockSpec(memory_space=pltpu.HBM)


params = pltpu.CompilerParams(vmem_limit_bytes=40 * 1024 * 1024)


def call(kernel, ins, outs, name, scalars=0, scratch=()):
    return pl.pallas_call(
        kernel,
        out_shape=[
            jax.ShapeDtypeStruct(s, f32) if isinstance(s, tuple) else jax.ShapeDtypeStruct(s.shape, s.dtype)
            for s in outs
        ],
        in_specs=[smem] * scalars + [vmem] * (len(ins) - scalars),
        out_specs=[vmem] * len(outs),
        scratch_shapes=list(scratch),
        compiler_params=params,
        name=name,
    )(*ins)


def tell(arrays, slices, cols):
    return pl.pallas_call(
        tell_kernel,
        out_shape=jax.ShapeDtypeStruct((slices, told, cols), f32),
        in_specs=[hbm] * len(arrays),
        out_specs=vmem,
        scratch_shapes=[pltpu.VMEM(a.shape, a.dtype) for a in arrays]
        + [pltpu.SemaphoreType.DMA((len(arrays),))],
        compiler_params=pltpu.CompilerParams(vmem_limit_bytes=65_000_000),
        name="tell",
    )(*arrays)


def swap(values, axis):
    pairs = values.reshape(values.shape[0] // 2, 2, 128)
    return lax.all_to_all(pairs, axis, 0, 0, tiled=True).reshape(values.shape)


def body(iterate, residual, direction, sensitivity, sampling, edge_weight):
    slabs = lax.axis_size(slab_axes)
    frames = lax.axis_size("coil")
    zdim, cols = direction.shape[2], direction.shape[4]

    sens = jnp.swapaxes(sensitivity, 2, 3)
    d = jnp.swapaxes(direction, 2, 3)[:, 0]
    r = jnp.swapaxes(residual, 2, 3)[:, 0]
    x = jnp.swapaxes(iterate, 2, 3)[:, 0]
    w = jnp.swapaxes(edge_weight, 1, 2)[0]

    cos, sin = dft_tables(cols)
    sizes = [lax.axis_size(a) for a in slab_axes]
    order = [slab_axes.index(a) for a in swap_axes]
    by_slab = np.arange(cols).reshape(*sizes, rows).transpose(3, *order).reshape(-1)
    natural = jnp.asarray(np.concatenate([cos, sin], axis=0))
    forward = jnp.asarray(np.concatenate([cos[:, by_slab], sin[:, by_slab]], axis=0))
    inverse = jnp.asarray(np.concatenate([cos[by_slab], sin[by_slab]], axis=0))
    wide = jnp.asarray(np.concatenate([cos, sin], axis=1))

    place = jnp.stack(
        [lax.axis_index(swap_axes), lax.axis_index(slab_axes), jnp.int32(slabs), lax.axis_index("coil")]
    ).astype(jnp.int32)
    mine = lax.all_to_all(tell((sens, d, w), zdim, cols), "coil", 0, 0, tiled=True)
    (natural,) = call(table_kernel, (natural,), [natural], "table")

    lines = slabs * message
    (spectrum,) = call(images_kernel, (mine, natural), [(lines, 128)], "images")
    spectrum = swap(spectrum, swap_axes)
    last, first = call(edges_kernel, (mine,), [(frames, 3, cols), (frames, 2, cols)], "edges")
    up = [(i, i + 1) for i in range(slabs - 1)]
    before = lax.ppermute(last, slab_axes, up)
    after = lax.ppermute(first, slab_axes, [(j, i) for i, j in up])
    (mask,) = call(mask_kernel, (place, sampling), [(cols // 128, cols, 128)], "mask", 1)
    own, *others = call(
        later_kernel,
        (place, d, r, w),
        [(told_later, cols)] * frames,
        "later",
        1,
        [pltpu.VMEM((told_later, zdim, cols), f32)],
    )
    later = [own]
    for k, other in enumerate(others, 1):
        later.append(lax.ppermute(other, "coil", [(i, (i + k) % frames) for i in range(frames)]))
    six = (frames, 2 * rows, cols)
    smooth, rest = call(
        smooth_kernel,
        (place, mine, before, after, *later),
        [six, six],
        "smooth",
        1,
        [pltpu.VMEM((frames, told_later, cols), f32)],
    )
    spectrum, smooth, rest = lax.optimization_barrier((spectrum, smooth, rest))
    (back,) = call(
        middle_kernel, (spectrum, mask, forward, inverse), [(lines, 128)], "middle"
    )
    back = swap(back, swap_axes)
    applied, parts = call(
        combine_kernel,
        (back, mine, smooth, rest, wide),
        [(frames, 8, cols), (slabs, 1, 128)],
        "combine",
    )
    parts = lax.all_to_all(parts, slab_axes, 0, 0, tiled=True)
    (applied,) = call(join_kernel, (parts, applied), [applied], "join")
    applied = lax.all_to_all(applied, "coil", 0, 0, tiled=True)

    flat = (2 * rows, zdim, cols)
    x, r, d = (v.reshape(flat) for v in (x, r, d))
    new_x, new_r, new_d, norm = call(
        finish_kernel, (applied, x, r, d), [flat, flat, flat, (1, 128)], "finish"
    )

    def restore(values):
        return jnp.swapaxes(values.reshape(2, 1, rows, zdim, cols), 2, 3)

    return restore(new_x), restore(new_r), restore(new_d), norm[0, 0]


def solution(mesh):
    fine = Mesh(mesh.devices.reshape(8, 8, 2, 4), ("z", "y", "core", "coil"))
    image = P(None, "coil", None, slab_axes, None)
    return jax.shard_map(
        body,
        mesh=fine,
        in_specs=(image, image, image, image, P(), P("coil", None, slab_axes, None)),
        out_specs=(image, image, image, P()),
        check_vma=False,
    )
```

```python
import math

import jax
import jax.numpy as jnp
import ml_dtypes
import numpy as np
from jax import lax
from jax.experimental import pallas as pl
from jax.experimental.pallas import tpu as pltpu
from jax.sharding import Mesh
from jax.sharding import PartitionSpec as P

smooth_scale = 0.05
slab_axes = ("z", "y", "core")
swap_axes = ("z", "core", "y")
f32 = jnp.float32
bf16 = jnp.bfloat16

message = 18

rows, coils = 3, 8
at_direction = 2 * rows * coils
at_edge = at_direction + 2 * rows
told = at_edge + 2
at_smooth = 2 * rows
at_weight = 4 * rows
told_later = 16


def dft_tables(length):
    counter = np.arange(length, dtype=np.int64)
    phases = (counter[:, None] * counter[None, :]) % length
    angles = phases.astype(np.float32) * np.float32(2.0 * math.pi / length)
    unit_norm = np.float32(1.0 / math.sqrt(length))
    wide = angles.astype(np.float64)
    cos = np.cos(wide).astype(np.float32) * unit_norm
    sin = np.sin(wide).astype(np.float32) * unit_norm
    return cos.astype(ml_dtypes.bfloat16), sin.astype(ml_dtypes.bfloat16)


def split(values):
    upper = values.astype(bf16)
    return upper, (values - upper.astype(f32)).astype(bf16)


def mm(a, b, contract):
    return lax.dot_general(a, b, (contract, ((), ())), preferred_element_type=f32)


def staggered(count, first, second):
    held, results = first(0), []
    for i in range(count):
        ahead = first(i + 1) if i + 1 < count else None
        results.append(second(i, held))
        held = ahead
    return results


def sens_rows(all_ref, part, row):
    at = (part * rows + row) * coils
    return jnp.concatenate([all_ref[k, at : at + coils] for k in range(all_ref.shape[0])], axis=0)


def tell_kernel(*refs):
    sources, out_ref, held, done = refs[:3], refs[3], refs[4:7], refs[7]
    copies = [pltpu.make_async_copy(sources[i], held[i], done.at[i]) for i in range(3)]
    for copy in copies:
        copy.start()
    for copy in copies:
        copy.wait()
    sens_ref, direction_ref, weight_ref = held
    slices, _, cols = out_ref.shape

    def put(row, values):
        for z in range(slices):
            out_ref[z, row : row + 1] = values[z : z + 1]

    for p in range(2):
        for r in range(rows):
            i = p * rows + r
            tiles = [sens_ref[p, c, r].astype(f32) for c in range(coils)]
            for z in range(slices):
                out_ref[z, i * coils : (i + 1) * coils] = jnp.concatenate(
                    [t[z : z + 1] for t in tiles], axis=0
                )
            put(at_direction + i, direction_ref[p, r])
    put(at_edge, weight_ref[rows - 1].astype(f32))
    put(at_edge + 1, jnp.zeros((slices, cols), f32))


def later_kernel(place_ref, direction_ref, residual_ref, weight_ref, *refs):
    out_refs, held_ref = refs[:-1], refs[-1]
    plane, planes = place_ref[3], len(out_refs)
    cols = direction_ref.shape[3]
    zero_slice = jnp.zeros((1, cols), f32)
    for r in range(rows):
        weight = weight_ref[r].astype(f32)
        held_ref[at_weight + r] = weight
        for p in range(2):
            i = p * rows + r
            v = direction_ref[p, r]
            held_ref[i] = residual_ref[p, r]
            flux = weight[:-1] * (v[1:] - v[:-1])
            held_ref[at_smooth + i] = jnp.concatenate([zero_slice, flux], axis=0) - jnp.concatenate(
                [flux, zero_slice], axis=0
            )
    for k in range(planes):
        z = lax.rem(plane + k, planes)
        for i in range(at_weight + rows):
            out_refs[k][i : i + 1] = held_ref[i, pl.ds(z, 1), :]
        out_refs[k][at_weight + rows :] = jnp.zeros((told_later - at_weight - rows, cols), f32)


def table_kernel(table_ref, out_ref):
    out_ref[...] = table_ref[...]


def images_kernel(all_ref, table_ref, out_ref):
    frames, _, cols = all_ref.shape
    table = table_ref[...]
    table = jnp.concatenate([table, table], axis=1)
    half = table.shape[0] // 2
    groups = half // 128

    def forward(r):
        s_re, s_im = sens_rows(all_ref, 0, r), sens_rows(all_ref, 1, r)
        real, imag = [], []
        for f in range(frames):
            at = at_direction + r
            d_re = jnp.broadcast_to(all_ref[f, at : at + 1], s_re.shape)
            d_im = jnp.broadcast_to(all_ref[f, at + rows : at + rows + 1], s_re.shape)
            real.append(s_re * d_re - s_im * d_im)
            imag.append(s_re * d_im + s_im * d_re)
        upper, lower = split(jnp.concatenate(real + imag, axis=0))
        return mm(table, jnp.concatenate([upper, lower], axis=1), ((1,), (1,)))

    def store(r, got):
        re = got[:half, :128] + got[half:, 128:]
        im = got[:half, 128:] - got[half:, :128]
        for j in range(groups):
            at = (j * rows + r) * 2
            out_ref[pl.ds(at, 128, stride=message), :] = re[j * 128 : (j + 1) * 128]
            out_ref[pl.ds(at + 1, 128, stride=message), :] = im[j * 128 : (j + 1) * 128]

    staggered(rows, forward, store)


def mask_kernel(place_ref, sampling_ref, out_ref):
    frames, full, cols = sampling_ref.shape
    groups = cols // 128
    lane = lax.broadcasted_iota(jnp.int32, (cols, cols), 1)
    freq = lax.broadcasted_iota(jnp.int32, (cols, cols), 0)
    wanted = (lane // 128) * 128 + place_ref[0]
    total = jnp.zeros((full, cols), f32)
    for f in range(frames):
        mine = (freq == wanted) & ((lane % 128) // (128 // frames) == f)
        chosen = jnp.where(mine, 1.0, 0.0).astype(bf16)
        total += mm(sampling_ref[f].astype(f32).astype(bf16), chosen, ((1,), (0,)))
    for j in range(groups):
        out_ref[j] = total[:, j * 128 : (j + 1) * 128]


def edges_kernel(all_ref, last_ref, first_ref):
    for f in range(all_ref.shape[0]):
        for p in range(2):
            at = at_direction + p * rows
            last_ref[f, p : p + 1] = all_ref[f, at + rows - 1 : at + rows]
            first_ref[f, p : p + 1] = all_ref[f, at : at + 1]
        last_ref[f, 2:3] = all_ref[f, at_edge : at_edge + 1]


def smooth_kernel(place_ref, all_ref, before_ref, after_ref, *refs):
    later_refs, out_ref, residual_ref, later_ref = refs[:-3], *refs[-3:]
    slab, slabs, plane = place_ref[1], place_ref[2], place_ref[3]
    frames, _, cols = all_ref.shape
    for k in range(frames):
        later_ref[lax.rem(plane + frames - k, frames)] = later_refs[k][...]
    residual_ref[...] = later_ref[:, : 2 * rows]
    has_next_row = jnp.where(slab < slabs - 1, 1.0, 0.0)
    has_previous_row = jnp.where(slab > 0, 1.0, 0.0)
    zero_col = jnp.zeros((rows, 1), f32)
    for p in range(2):
        at = at_direction + p * rows
        from_frame = None
        for f in range(frames):
            v = all_ref[f, at : at + rows]
            weight = later_ref[f, at_weight : at_weight + rows]
            term = later_ref[f, at_smooth + p * rows : at_smooth + (p + 1) * rows]
            if from_frame is not None:
                term = term + from_frame
            if f < frames - 1:
                from_frame = weight * (all_ref[f + 1, at : at + rows] - v)
                term = term - from_frame
            flux = weight[:, :-1] * (v[:, 1:] - v[:, :-1])
            term += jnp.concatenate([zero_col, flux], axis=1)
            term -= jnp.concatenate([flux, zero_col], axis=1)
            previous = before_ref[f, p : p + 1]
            following = after_ref[f, p : p + 1]
            first = (before_ref[f, 2:3] * has_previous_row) * (v[0:1] - previous)
            inner = weight[:-1] * (v[1:] - v[:-1])
            final = (weight[-1:] * has_next_row) * (following - v[-1:])
            term += jnp.concatenate([first, inner], axis=0)
            term -= jnp.concatenate([inner, final], axis=0)
            out_ref[f, p * rows : (p + 1) * rows] = smooth_scale * term


def middle_kernel(in_ref, mask_ref, forward_ref, inverse_ref, out_ref):
    groups = mask_ref.shape[0]
    forward = forward_ref[...]
    forward = jnp.concatenate([forward, forward], axis=1)
    inverse = inverse_ref[...]
    inverse = jnp.concatenate([inverse, inverse], axis=1)
    half = forward.shape[0] // 2

    def gather(j):
        parts = []
        for r in range(rows):
            at = (j * rows + r) * 2
            re = in_ref[pl.ds(at, 128, stride=message), :]
            im = in_ref[pl.ds(at + 1, 128, stride=message), :]
            parts.append(jnp.concatenate([re, im], axis=1))
        upper, lower = split(jnp.concatenate(parts, axis=0))
        return mm(forward, jnp.concatenate([upper, lower], axis=0), ((1,), (0,)))

    def sample(j, got):
        mask = mask_ref[j]
        re = (got[:half, :128] + got[half:, 128:]) * mask
        im = (got[:half, 128:] - got[half:, :128]) * mask
        upper, lower = split(jnp.concatenate([re, im], axis=1))
        back = mm(inverse, jnp.concatenate([upper, lower], axis=0), ((1,), (0,)))
        store(j, back)

    def store(j, got):
        re = got[:half, :128] - got[half:, 128:]
        im = got[:half, 128:] + got[half:, :128]
        for r in range(rows):
            at = (r * groups + j) * 2
            out_ref[pl.ds(at, 128, stride=message), :] = re[r * 128 : (r + 1) * 128]
            out_ref[pl.ds(at + 1, 128, stride=message), :] = im[r * 128 : (r + 1) * 128]

    staggered(groups, gather, sample)


def whole(values):
    return jnp.sum(jnp.sum(values, axis=0, keepdims=True), axis=1, keepdims=True)


def in_lanes(values):
    lane = lax.broadcasted_iota(jnp.int32, (1, 128), 1)
    row = jnp.zeros((1, 128), f32)
    for i, value in enumerate(values):
        row = jnp.where(lane == i, value, row)
    return row


def share(value, weight):
    return jnp.where(weight > 0, value / jnp.where(weight > 0, weight, 1.0), 0.0)


def combine_kernel(in_ref, all_ref, smooth_ref, residual_ref, table_ref, applied_ref, out_ref):
    frames, _, cols = all_ref.shape
    table = table_ref[...]
    table = jnp.concatenate([table, table], axis=0)
    groups = cols // 128
    span = 128 // frames
    zero = jnp.zeros((1, cols), f32)

    def backward(r):
        real, imag = [], []
        for j in range(groups):
            at = (r * groups + j) * 2
            real.append(in_ref[pl.ds(at, 128, stride=message), :].T)
            imag.append(in_ref[pl.ds(at + 1, 128, stride=message), :].T)
        both = jnp.concatenate(
            [jnp.concatenate(real, axis=1), jnp.concatenate(imag, axis=1)], axis=0
        )
        upper, lower = split(both)
        return mm(jnp.concatenate([upper, lower], axis=1), table, ((1,), (0,)))

    def add_coils(r, got):
        re = got[:128, :cols] - got[128:, cols:]
        im = got[128:, :cols] + got[:128, cols:]
        s_re, s_im = sens_rows(all_ref, 0, r), sens_rows(all_ref, 1, r)
        for f in range(frames):
            b_re = re[f * span : (f + 1) * span]
            b_im = im[f * span : (f + 1) * span]
            for p, t in enumerate((s_re * b_re + s_im * b_im, s_re * b_im - s_im * b_re)):
                i = p * rows + r
                total = jnp.sum(t, axis=0, keepdims=True)
                applied_ref[f, i : i + 1] = total + smooth_ref[f, i : i + 1]

    staggered(rows, backward, add_coils)
    six = 2 * rows
    zero = jnp.zeros((six, cols), f32)
    norm, curvature, size, cross, rest = zero, zero, zero, zero, zero
    for f in range(frames):
        value = applied_ref[f, 0:six]
        r = residual_ref[f]
        norm += r * r
        curvature += all_ref[f, at_direction : at_direction + six] * value
        size += value * value
        cross += r * value
    size = whole(size)
    ratio = share(whole(cross), size)
    for f in range(frames):
        left = residual_ref[f] - ratio * applied_ref[f, 0:six]
        rest += left * left
        applied_ref[f, six:] = jnp.zeros((applied_ref.shape[1] - six, cols), f32)
    row = in_lanes([whole(norm), whole(curvature), size, ratio, whole(rest)])
    out_ref[...] = jnp.broadcast_to(row[None], out_ref.shape)


def joined(parts):
    size, ratio = parts[:, 2:3], parts[:, 3:4]
    norm, curvature = whole(parts[:, 0:1]), whole(parts[:, 1:2])
    all_size = whole(size)
    all_ratio = share(whole(size * ratio), all_size)
    away = ratio - all_ratio
    rest = whole(parts[:, 4:5] + (size * away) * away)
    return norm, curvature, all_size, all_ratio, rest


def join_kernel(parts_ref, applied_ref, out_ref):
    row = in_lanes(joined(parts_ref[:, 0, :]))
    out_ref[...] = applied_ref[...]
    for f in range(out_ref.shape[0]):
        out_ref[f, 2 * rows : 2 * rows + 1, 0:128] = row


def finish_kernel(
    all_ref, iterate_ref, residual_ref, direction_ref, new_iterate_ref, new_residual_ref, new_direction_ref, norm_ref
):
    slices = all_ref.shape[0]
    parts = [all_ref[z, 2 * rows : 2 * rows + 1, 0:128] for z in range(slices)]
    old_norm, curvature, size, ratio, rest = joined(jnp.concatenate(parts, axis=0))
    step = old_norm / curvature
    away = ratio - step
    new_norm = rest + (size * away) * away
    turn = new_norm / old_norm
    for i in range(direction_ref.shape[0]):
        d = direction_ref[i]
        applied = jnp.concatenate([all_ref[z, i : i + 1] for z in range(slices)], axis=0)
        fresh = residual_ref[i] - step * applied
        new_iterate_ref[i] = iterate_ref[i] + step * d
        new_residual_ref[i] = fresh
        new_direction_ref[i] = fresh + turn * d
    norm_ref[...] = jnp.broadcast_to(new_norm, norm_ref.shape)


vmem = pl.BlockSpec(memory_space=pltpu.VMEM)
smem = pl.BlockSpec(memory_space=pltpu.SMEM)
hbm = pl.BlockSpec(memory_space=pltpu.HBM)


params = pltpu.CompilerParams(vmem_limit_bytes=40 * 1024 * 1024)


def call(kernel, ins, outs, name, scalars=0, scratch=()):
    return pl.pallas_call(
        kernel,
        out_shape=[
            jax.ShapeDtypeStruct(s, f32) if isinstance(s, tuple) else jax.ShapeDtypeStruct(s.shape, s.dtype)
            for s in outs
        ],
        in_specs=[smem] * scalars + [vmem] * (len(ins) - scalars),
        out_specs=[vmem] * len(outs),
        scratch_shapes=list(scratch),
        compiler_params=params,
        name=name,
    )(*ins)


def tell(arrays, slices, cols):
    return pl.pallas_call(
        tell_kernel,
        out_shape=jax.ShapeDtypeStruct((slices, told, cols), f32),
        in_specs=[hbm] * len(arrays),
        out_specs=vmem,
        scratch_shapes=[pltpu.VMEM(a.shape, a.dtype) for a in arrays]
        + [pltpu.SemaphoreType.DMA((len(arrays),))],
        compiler_params=pltpu.CompilerParams(vmem_limit_bytes=65_000_000),
        name="tell",
    )(*arrays)


def swap(values, axis):
    pairs = values.reshape(values.shape[0] // 2, 2, 128)
    return lax.all_to_all(pairs, axis, 0, 0, tiled=True).reshape(values.shape)


def body(iterate, residual, direction, sensitivity, sampling, edge_weight):
    slabs = lax.axis_size(slab_axes)
    frames = lax.axis_size("coil")
    zdim, cols = direction.shape[2], direction.shape[4]

    sens = jnp.swapaxes(sensitivity, 2, 3)
    d = jnp.swapaxes(direction, 2, 3)[:, 0]
    r = jnp.swapaxes(residual, 2, 3)[:, 0]
    x = jnp.swapaxes(iterate, 2, 3)[:, 0]
    w = jnp.swapaxes(edge_weight, 1, 2)[0]

    cos, sin = dft_tables(cols)
    sizes = [lax.axis_size(a) for a in slab_axes]
    order = [slab_axes.index(a) for a in swap_axes]
    by_slab = np.arange(cols).reshape(*sizes, rows).transpose(3, *order).reshape(-1)
    natural = jnp.asarray(np.concatenate([cos, sin], axis=0))
    forward = jnp.asarray(np.concatenate([cos[:, by_slab], sin[:, by_slab]], axis=0))
    inverse = jnp.asarray(np.concatenate([cos[by_slab], sin[by_slab]], axis=0))
    wide = jnp.asarray(np.concatenate([cos, sin], axis=1))

    place = jnp.stack(
        [lax.axis_index(swap_axes), lax.axis_index(slab_axes), jnp.int32(slabs), lax.axis_index("coil")]
    ).astype(jnp.int32)
    mine = lax.all_to_all(tell((sens, d, w), zdim, cols), "coil", 0, 0, tiled=True)
    (natural,) = call(table_kernel, (natural,), [natural], "table")

    lines = slabs * message
    (spectrum,) = call(images_kernel, (mine, natural), [(lines, 128)], "images")
    spectrum = swap(spectrum, swap_axes)
    last, first = call(edges_kernel, (mine,), [(frames, 3, cols), (frames, 2, cols)], "edges")
    up = [(i, i + 1) for i in range(slabs - 1)]
    before = lax.ppermute(last, slab_axes, up)
    after = lax.ppermute(first, slab_axes, [(j, i) for i, j in up])
    (mask,) = call(mask_kernel, (place, sampling), [(cols // 128, cols, 128)], "mask", 1)
    own, *others = call(
        later_kernel,
        (place, d, r, w),
        [(told_later, cols)] * frames,
        "later",
        1,
        [pltpu.VMEM((told_later, zdim, cols), f32)],
    )
    later = [own]
    for k, other in enumerate(others, 1):
        later.append(lax.ppermute(other, "coil", [(i, (i + k) % frames) for i in range(frames)]))
    six = (frames, 2 * rows, cols)
    smooth, rest = call(
        smooth_kernel,
        (place, mine, before, after, *later),
        [six, six],
        "smooth",
        1,
        [pltpu.VMEM((frames, told_later, cols), f32)],
    )
    spectrum, smooth, rest = lax.optimization_barrier((spectrum, smooth, rest))
    (back,) = call(
        middle_kernel, (spectrum, mask, forward, inverse), [(lines, 128)], "middle"
    )
    back = swap(back, swap_axes)
    applied, parts = call(
        combine_kernel,
        (back, mine, smooth, rest, wide),
        [(frames, 8, cols), (slabs, 1, 128)],
        "combine",
    )
    turned = np.roll(np.arange(slabs).reshape(sizes), [n // 2 for n in sizes[:2]], (0, 1))
    turned = [int(v) for v in turned.reshape(-1)]
    parts = lax.all_to_all(parts, slab_axes, 0, 0, axis_index_groups=[turned], tiled=True)
    (applied,) = call(join_kernel, (parts, applied), [applied], "join")
    applied = lax.all_to_all(applied, "coil", 0, 0, tiled=True)

    flat = (2 * rows, zdim, cols)
    x, r, d = (v.reshape(flat) for v in (x, r, d))
    new_x, new_r, new_d, norm = call(
        finish_kernel, (applied, x, r, d), [flat, flat, flat, (1, 128)], "finish"
    )

    def restore(values):
        return jnp.swapaxes(values.reshape(2, 1, rows, zdim, cols), 2, 3)

    return restore(new_x), restore(new_r), restore(new_d), norm[0, 0]


def solution(mesh):
    fine = Mesh(mesh.devices.reshape(8, 8, 2, 4), ("z", "y", "core", "coil"))
    image = P(None, "coil", None, slab_axes, None)
    return jax.shard_map(
        body,
        mesh=fine,
        in_specs=(image, image, image, image, P(), P("coil", None, slab_axes, None)),
        out_specs=(image, image, image, P()),
        check_vma=False,
    )
```

```python
import math

import jax
import jax.numpy as jnp
import ml_dtypes
import numpy as np
from jax import lax
from jax.experimental import pallas as pl
from jax.experimental.pallas import tpu as pltpu
from jax.sharding import Mesh
from jax.sharding import PartitionSpec as P

smooth_scale = 0.05
slab_axes = ("z", "y", "core")
swap_axes = ("z", "core", "y")
f32 = jnp.float32
bf16 = jnp.bfloat16

message = 18

rows, coils = 3, 8
at_direction = 2 * rows * coils
at_edge = at_direction + 2 * rows
told = at_edge + 2
at_smooth = 2 * rows
at_weight = 4 * rows
told_later = 16


def dft_tables(length):
    counter = np.arange(length, dtype=np.int64)
    phases = (counter[:, None] * counter[None, :]) % length
    angles = phases.astype(np.float32) * np.float32(2.0 * math.pi / length)
    unit_norm = np.float32(1.0 / math.sqrt(length))
    wide = angles.astype(np.float64)
    cos = np.cos(wide).astype(np.float32) * unit_norm
    sin = np.sin(wide).astype(np.float32) * unit_norm
    return cos.astype(ml_dtypes.bfloat16), sin.astype(ml_dtypes.bfloat16)


def split(values):
    upper = values.astype(bf16)
    return upper, (values - upper.astype(f32)).astype(bf16)


def mm(a, b, contract):
    return lax.dot_general(a, b, (contract, ((), ())), preferred_element_type=f32)


def staggered(count, first, second):
    held, results = first(0), []
    for i in range(count):
        ahead = first(i + 1) if i + 1 < count else None
        results.append(second(i, held))
        held = ahead
    return results


def sens_rows(all_ref, part, row):
    at = (part * rows + row) * coils
    return jnp.concatenate([all_ref[k, at : at + coils] for k in range(all_ref.shape[0])], axis=0)


def tell_kernel(*refs):
    sources, out_ref, held, done = refs[:3], refs[3], refs[4:7], refs[7]
    copies = [pltpu.make_async_copy(sources[i], held[i], done.at[i]) for i in range(3)]
    for copy in copies:
        copy.start()
    for copy in copies:
        copy.wait()
    sens_ref, direction_ref, weight_ref = held
    slices, _, cols = out_ref.shape

    def put(row, values):
        for z in range(slices):
            out_ref[z, row : row + 1] = values[z : z + 1]

    for p in range(2):
        for r in range(rows):
            i = p * rows + r
            tiles = [sens_ref[p, c, r].astype(f32) for c in range(coils)]
            for z in range(slices):
                out_ref[z, i * coils : (i + 1) * coils] = jnp.concatenate(
                    [t[z : z + 1] for t in tiles], axis=0
                )
            put(at_direction + i, direction_ref[p, r])
    put(at_edge, weight_ref[rows - 1].astype(f32))
    put(at_edge + 1, jnp.zeros((slices, cols), f32))


def later_kernel(place_ref, direction_ref, residual_ref, weight_ref, *refs):
    out_refs, held_ref = refs[:-1], refs[-1]
    plane, planes = place_ref[3], len(out_refs)
    cols = direction_ref.shape[3]
    zero_slice = jnp.zeros((1, cols), f32)
    for r in range(rows):
        weight = weight_ref[r].astype(f32)
        held_ref[at_weight + r] = weight
        for p in range(2):
            i = p * rows + r
            v = direction_ref[p, r]
            held_ref[i] = residual_ref[p, r]
            flux = weight[:-1] * (v[1:] - v[:-1])
            held_ref[at_smooth + i] = jnp.concatenate([zero_slice, flux], axis=0) - jnp.concatenate(
                [flux, zero_slice], axis=0
            )
    for k in range(planes):
        z = lax.rem(plane + k, planes)
        for i in range(at_weight + rows):
            out_refs[k][i : i + 1] = held_ref[i, pl.ds(z, 1), :]
        out_refs[k][at_weight + rows :] = jnp.zeros((told_later - at_weight - rows, cols), f32)


def table_kernel(table_ref, out_ref):
    out_ref[...] = table_ref[...]


def images_kernel(all_ref, table_ref, out_ref):
    frames, _, cols = all_ref.shape
    table = table_ref[...]
    table = jnp.concatenate([table, table], axis=1)
    half = table.shape[0] // 2
    groups = half // 128

    def forward(r):
        s_re, s_im = sens_rows(all_ref, 0, r), sens_rows(all_ref, 1, r)
        real, imag = [], []
        for f in range(frames):
            at = at_direction + r
            d_re = jnp.broadcast_to(all_ref[f, at : at + 1], s_re.shape)
            d_im = jnp.broadcast_to(all_ref[f, at + rows : at + rows + 1], s_re.shape)
            real.append(s_re * d_re - s_im * d_im)
            imag.append(s_re * d_im + s_im * d_re)
        upper, lower = split(jnp.concatenate(real + imag, axis=0))
        return mm(table, jnp.concatenate([upper, lower], axis=1), ((1,), (1,)))

    def store(r, got):
        re = got[:half, :128] + got[half:, 128:]
        im = got[:half, 128:] - got[half:, :128]
        for j in range(groups):
            at = (j * rows + r) * 2
            out_ref[pl.ds(at, 128, stride=message), :] = re[j * 128 : (j + 1) * 128]
            out_ref[pl.ds(at + 1, 128, stride=message), :] = im[j * 128 : (j + 1) * 128]

    staggered(rows, forward, store)


def mask_kernel(place_ref, sampling_ref, out_ref):
    frames, full, cols = sampling_ref.shape
    groups = cols // 128
    lane = lax.broadcasted_iota(jnp.int32, (cols, cols), 1)
    freq = lax.broadcasted_iota(jnp.int32, (cols, cols), 0)
    wanted = (lane // 128) * 128 + place_ref[0]
    total = jnp.zeros((full, cols), f32)
    for f in range(frames):
        mine = (freq == wanted) & ((lane % 128) // (128 // frames) == f)
        chosen = jnp.where(mine, 1.0, 0.0).astype(bf16)
        total += mm(sampling_ref[f].astype(f32).astype(bf16), chosen, ((1,), (0,)))
    for j in range(groups):
        out_ref[j] = total[:, j * 128 : (j + 1) * 128]


def edges_kernel(all_ref, last_ref, first_ref):
    for f in range(all_ref.shape[0]):
        for p in range(2):
            at = at_direction + p * rows
            last_ref[f, p : p + 1] = all_ref[f, at + rows - 1 : at + rows]
            first_ref[f, p : p + 1] = all_ref[f, at : at + 1]
        last_ref[f, 2:3] = all_ref[f, at_edge : at_edge + 1]


def smooth_kernel(place_ref, all_ref, before_ref, after_ref, *refs):
    later_refs, out_ref, residual_ref, later_ref = refs[:-3], *refs[-3:]
    slab, slabs, plane = place_ref[1], place_ref[2], place_ref[3]
    frames, _, cols = all_ref.shape
    for k in range(frames):
        later_ref[lax.rem(plane + frames - k, frames)] = later_refs[k][...]
    residual_ref[...] = later_ref[:, : 2 * rows]
    has_next_row = jnp.where(slab < slabs - 1, 1.0, 0.0)
    has_previous_row = jnp.where(slab > 0, 1.0, 0.0)
    zero_col = jnp.zeros((rows, 1), f32)
    for p in range(2):
        at = at_direction + p * rows
        from_frame = None
        for f in range(frames):
            v = all_ref[f, at : at + rows]
            weight = later_ref[f, at_weight : at_weight + rows]
            term = later_ref[f, at_smooth + p * rows : at_smooth + (p + 1) * rows]
            if from_frame is not None:
                term = term + from_frame
            if f < frames - 1:
                from_frame = weight * (all_ref[f + 1, at : at + rows] - v)
                term = term - from_frame
            flux = weight[:, :-1] * (v[:, 1:] - v[:, :-1])
            term += jnp.concatenate([zero_col, flux], axis=1)
            term -= jnp.concatenate([flux, zero_col], axis=1)
            previous = before_ref[f, p : p + 1]
            following = after_ref[f, p : p + 1]
            first = (before_ref[f, 2:3] * has_previous_row) * (v[0:1] - previous)
            inner = weight[:-1] * (v[1:] - v[:-1])
            final = (weight[-1:] * has_next_row) * (following - v[-1:])
            term += jnp.concatenate([first, inner], axis=0)
            term -= jnp.concatenate([inner, final], axis=0)
            out_ref[f, p * rows : (p + 1) * rows] = smooth_scale * term


def middle_kernel(in_ref, mask_ref, forward_ref, inverse_ref, out_ref):
    groups = mask_ref.shape[0]
    forward = forward_ref[...]
    forward = jnp.concatenate([forward, forward], axis=1)
    inverse = inverse_ref[...]
    inverse = jnp.concatenate([inverse, inverse], axis=1)
    half = forward.shape[0] // 2

    def gather(j):
        parts = []
        for r in range(rows):
            at = (j * rows + r) * 2
            re = in_ref[pl.ds(at, 128, stride=message), :]
            im = in_ref[pl.ds(at + 1, 128, stride=message), :]
            parts.append(jnp.concatenate([re, im], axis=1))
        upper, lower = split(jnp.concatenate(parts, axis=0))
        return mm(forward, jnp.concatenate([upper, lower], axis=0), ((1,), (0,)))

    def sample(j, got):
        mask = mask_ref[j]
        re = (got[:half, :128] + got[half:, 128:]) * mask
        im = (got[:half, 128:] - got[half:, :128]) * mask
        upper, lower = split(jnp.concatenate([re, im], axis=1))
        back = mm(inverse, jnp.concatenate([upper, lower], axis=0), ((1,), (0,)))
        store(j, back)

    def store(j, got):
        re = got[:half, :128] - got[half:, 128:]
        im = got[:half, 128:] + got[half:, :128]
        for r in range(rows):
            at = (r * groups + j) * 2
            out_ref[pl.ds(at, 128, stride=message), :] = re[r * 128 : (r + 1) * 128]
            out_ref[pl.ds(at + 1, 128, stride=message), :] = im[r * 128 : (r + 1) * 128]

    staggered(groups, gather, sample)


def whole(values):
    return jnp.sum(jnp.sum(values, axis=0, keepdims=True), axis=1, keepdims=True)


def in_lanes(values):
    lane = lax.broadcasted_iota(jnp.int32, (1, 128), 1)
    row = jnp.zeros((1, 128), f32)
    for i, value in enumerate(values):
        row = jnp.where(lane == i, value, row)
    return row


def share(value, weight):
    return jnp.where(weight > 0, value / jnp.where(weight > 0, weight, 1.0), 0.0)


def combine_kernel(in_ref, all_ref, smooth_ref, residual_ref, table_ref, applied_ref, out_ref):
    frames, _, cols = all_ref.shape
    table = table_ref[...]
    table = jnp.concatenate([table, table], axis=0)
    groups = cols // 128
    span = 128 // frames
    zero = jnp.zeros((1, cols), f32)

    def backward(r):
        real, imag = [], []
        for j in range(groups):
            at = (r * groups + j) * 2
            real.append(in_ref[pl.ds(at, 128, stride=message), :].T)
            imag.append(in_ref[pl.ds(at + 1, 128, stride=message), :].T)
        both = jnp.concatenate(
            [jnp.concatenate(real, axis=1), jnp.concatenate(imag, axis=1)], axis=0
        )
        upper, lower = split(both)
        return mm(jnp.concatenate([upper, lower], axis=1), table, ((1,), (0,)))

    def add_coils(r, got):
        re = got[:128, :cols] - got[128:, cols:]
        im = got[128:, :cols] + got[:128, cols:]
        s_re, s_im = sens_rows(all_ref, 0, r), sens_rows(all_ref, 1, r)
        for f in range(frames):
            b_re = re[f * span : (f + 1) * span]
            b_im = im[f * span : (f + 1) * span]
            for p, t in enumerate((s_re * b_re + s_im * b_im, s_re * b_im - s_im * b_re)):
                i = p * rows + r
                total = jnp.sum(t, axis=0, keepdims=True)
                applied_ref[f, i : i + 1] = total + smooth_ref[f, i : i + 1]

    staggered(rows, backward, add_coils)
    six = 2 * rows
    zero = jnp.zeros((six, cols), f32)
    norm, curvature, size, cross, rest = zero, zero, zero, zero, zero
    for f in range(frames):
        value = applied_ref[f, 0:six]
        r = residual_ref[f]
        norm += r * r
        curvature += all_ref[f, at_direction : at_direction + six] * value
        size += value * value
        cross += r * value
    size = whole(size)
    ratio = share(whole(cross), size)
    for f in range(frames):
        left = residual_ref[f] - ratio * applied_ref[f, 0:six]
        rest += left * left
        applied_ref[f, six:] = jnp.zeros((applied_ref.shape[1] - six, cols), f32)
    row = in_lanes([whole(norm), whole(curvature), size, ratio, whole(rest)])
    out_ref[...] = jnp.broadcast_to(row[None], out_ref.shape)


def joined(parts):
    size, ratio = parts[:, 2:3], parts[:, 3:4]
    norm, curvature = whole(parts[:, 0:1]), whole(parts[:, 1:2])
    all_size = whole(size)
    all_ratio = share(whole(size * ratio), all_size)
    away = ratio - all_ratio
    rest = whole(parts[:, 4:5] + (size * away) * away)
    return norm, curvature, all_size, all_ratio, rest


def join_kernel(parts_ref, applied_ref, out_ref):
    row = in_lanes(joined(parts_ref[:, 0, :]))
    out_ref[...] = applied_ref[...]
    for f in range(out_ref.shape[0]):
        out_ref[f, 2 * rows : 2 * rows + 1, 0:128] = row


def finish_kernel(
    all_ref, iterate_ref, residual_ref, direction_ref, new_iterate_ref, new_residual_ref, new_direction_ref, norm_ref
):
    slices = all_ref.shape[0]
    parts = [all_ref[z, 2 * rows : 2 * rows + 1, 0:128] for z in range(slices)]
    old_norm, curvature, size, ratio, rest = joined(jnp.concatenate(parts, axis=0))
    step = old_norm / curvature
    away = ratio - step
    new_norm = rest + (size * away) * away
    turn = new_norm / old_norm
    for i in range(direction_ref.shape[0]):
        d = direction_ref[i]
        applied = jnp.concatenate([all_ref[z, i : i + 1] for z in range(slices)], axis=0)
        fresh = residual_ref[i] - step * applied
        new_iterate_ref[i] = iterate_ref[i] + step * d
        new_residual_ref[i] = fresh
        new_direction_ref[i] = fresh + turn * d
    norm_ref[...] = jnp.broadcast_to(new_norm, norm_ref.shape)


vmem = pl.BlockSpec(memory_space=pltpu.VMEM)
smem = pl.BlockSpec(memory_space=pltpu.SMEM)
hbm = pl.BlockSpec(memory_space=pltpu.HBM)


params = pltpu.CompilerParams(vmem_limit_bytes=40 * 1024 * 1024)


def call(kernel, ins, outs, name, scalars=0, scratch=()):
    return pl.pallas_call(
        kernel,
        out_shape=[
            jax.ShapeDtypeStruct(s, f32) if isinstance(s, tuple) else jax.ShapeDtypeStruct(s.shape, s.dtype)
            for s in outs
        ],
        in_specs=[smem] * scalars + [vmem] * (len(ins) - scalars),
        out_specs=[vmem] * len(outs),
        scratch_shapes=list(scratch),
        compiler_params=params,
        name=name,
    )(*ins)


def tell(arrays, slices, cols):
    return pl.pallas_call(
        tell_kernel,
        out_shape=jax.ShapeDtypeStruct((slices, told, cols), f32),
        in_specs=[hbm] * len(arrays),
        out_specs=vmem,
        scratch_shapes=[pltpu.VMEM(a.shape, a.dtype) for a in arrays]
        + [pltpu.SemaphoreType.DMA((len(arrays),))],
        compiler_params=pltpu.CompilerParams(vmem_limit_bytes=65_000_000),
        name="tell",
    )(*arrays)


def swap(values, axis):
    pairs = values.reshape(values.shape[0] // 2, 2, 128)
    return lax.all_to_all(pairs, axis, 0, 0, tiled=True).reshape(values.shape)


def body(iterate, residual, direction, sensitivity, sampling, edge_weight):
    slabs = lax.axis_size(slab_axes)
    frames = lax.axis_size("coil")
    zdim, cols = direction.shape[2], direction.shape[4]

    sens = jnp.swapaxes(sensitivity, 2, 3)
    d = jnp.swapaxes(direction, 2, 3)[:, 0]
    r = jnp.swapaxes(residual, 2, 3)[:, 0]
    x = jnp.swapaxes(iterate, 2, 3)[:, 0]
    w = jnp.swapaxes(edge_weight, 1, 2)[0]

    cos, sin = dft_tables(cols)
    sizes = [lax.axis_size(a) for a in slab_axes]
    order = [slab_axes.index(a) for a in swap_axes]
    by_slab = np.arange(cols).reshape(*sizes, rows).transpose(3, *order).reshape(-1)
    natural = jnp.asarray(np.concatenate([cos, sin], axis=0))
    forward = jnp.asarray(np.concatenate([cos[:, by_slab], sin[:, by_slab]], axis=0))
    inverse = jnp.asarray(np.concatenate([cos[by_slab], sin[by_slab]], axis=0))
    wide = jnp.asarray(np.concatenate([cos, sin], axis=1))

    place = jnp.stack(
        [lax.axis_index(swap_axes), lax.axis_index(slab_axes), jnp.int32(slabs), lax.axis_index("coil")]
    ).astype(jnp.int32)
    mine = lax.all_to_all(tell((sens, d, w), zdim, cols), "coil", 0, 0, tiled=True)
    (natural,) = call(table_kernel, (natural,), [natural], "table")

    lines = slabs * message
    (spectrum,) = call(images_kernel, (mine, natural), [(lines, 128)], "images")
    spectrum = swap(spectrum, swap_axes)
    last, first = call(edges_kernel, (mine,), [(frames, 3, cols), (frames, 2, cols)], "edges")
    up = [(i, i + 1) for i in range(slabs - 1)]
    before = lax.ppermute(last, slab_axes, up)
    after = lax.ppermute(first, slab_axes, [(j, i) for i, j in up])
    (mask,) = call(mask_kernel, (place, sampling), [(cols // 128, cols, 128)], "mask", 1)
    own, *others = call(
        later_kernel,
        (place, d, r, w),
        [(told_later, cols)] * frames,
        "later",
        1,
        [pltpu.VMEM((told_later, zdim, cols), f32)],
    )
    later = [own]
    for k, other in enumerate(others, 1):
        later.append(lax.ppermute(other, "coil", [(i, (i + k) % frames) for i in range(frames)]))
    six = (frames, 2 * rows, cols)
    smooth, rest = call(
        smooth_kernel,
        (place, mine, before, after, *later),
        [six, six],
        "smooth",
        1,
        [pltpu.VMEM((frames, told_later, cols), f32)],
    )
    spectrum, smooth, rest = lax.optimization_barrier((spectrum, smooth, rest))
    (back,) = call(
        middle_kernel, (spectrum, mask, forward, inverse), [(lines, 128)], "middle"
    )
    back = swap(back, swap_axes)
    applied, parts = call(
        combine_kernel,
        (back, mine, smooth, rest, wide),
        [(frames, 8, cols), (slabs, 1, 128)],
        "combine",
    )
    turned = np.roll(np.arange(slabs).reshape(sizes), [n // 2 for n in sizes[:2]], (0, 1))
    turned = [int(v) for v in turned[:, :, ::-1].reshape(-1)]
    parts = lax.all_to_all(parts, slab_axes, 0, 0, axis_index_groups=[turned], tiled=True)
    (applied,) = call(join_kernel, (parts, applied), [applied], "join")
    applied = lax.all_to_all(applied, "coil", 0, 0, tiled=True)

    flat = (2 * rows, zdim, cols)
    x, r, d = (v.reshape(flat) for v in (x, r, d))
    new_x, new_r, new_d, norm = call(
        finish_kernel, (applied, x, r, d), [flat, flat, flat, (1, 128)], "finish"
    )

    def restore(values):
        return jnp.swapaxes(values.reshape(2, 1, rows, zdim, cols), 2, 3)

    return restore(new_x), restore(new_r), restore(new_d), norm[0, 0]


def solution(mesh):
    fine = Mesh(mesh.devices.reshape(8, 8, 2, 4), ("z", "y", "core", "coil"))
    image = P(None, "coil", None, slab_axes, None)
    return jax.shard_map(
        body,
        mesh=fine,
        in_specs=(image, image, image, image, P(), P("coil", None, slab_axes, None)),
        out_specs=(image, image, image, P()),
        check_vma=False,
    )
```
